128 devices in a mesh: row: 8 (over x_lo, z), col: 16 (over y, x_hi, core).
Axes of the slice: x: 4 (x_hi: 2, x_lo: 2; x = x_hi * 2 + x_lo), y: 4, z: 4, core: 2. Of those that a mesh axis runs over, the one named last changes fastest.
Arguments:
- a_band: bfloat16 [512, 32, 128, 128], P(('row', 'col')), may hold values from -4 to 4
- a_mask: int32 [512, 32], P(('row', 'col')), may hold values 0 or 1
- b_band: bfloat16 [512, 32, 128, 128], P(('row', 'col')), may hold values from -4 to 4
- b_mask: int32 [512, 32], P(('row', 'col')), may hold values 0 or 1
Outputs:
- c_grid: bfloat16 [512, 64, 128, 128], P('row', 'col')
The draws below stay inside these ranges and needn't reach their ends.
All inputs are finite; a program needn't handle non-finite values. No bound on the sum of `a_mask` or of `b_mask` on one device may be relied on, other than what follows from the above.
Results may differ from the reference program's by a relative error of at most 0.001.
Values may be sent and summed in bfloat16 or wider, within the bound.
A program may use at most 192 MiB of HBM per device.

```python
import jax
import jax.numpy as jnp
from jax import lax

BLOCKS = 512
BS = 128
BAND = 32
STEPS = 4
N_ROW = 8
N_COL = 16


def place_ends(result, own_key, least, high):
    place = [jax.random.randint(jax.random.fold_in(own_key, axis), (), 0, length) for axis, length in enumerate(result.shape)]
    longest = result.shape.index(max(result.shape))
    neighbour = place[:longest] + [(place[longest] + 1) % result.shape[longest]] + place[longest + 1:]
    return result.at[tuple(place)].set(least).at[tuple(neighbour)].set(high)


def block_levels(rng, dims, split, least, top_value):
    def one(axis_at, blocks):
        heights = jax.random.uniform(jax.random.fold_in(jax.random.fold_in(rng, 6), axis_at), (blocks,), jnp.float32, least / len(split), top_value / len(split))
        return jnp.repeat(jnp.exp(heights), dims[axis_at] // blocks).reshape((-1,) + (1,) * (len(dims) - axis_at - 1))

    gain = one(*split[0])
    for cut in split[1:]:
        gain = gain * one(*cut)
    return gain


def scatter_about(own_key, shape, width, limit, split=(), kind=jnp.bfloat16):
    loudness = block_levels(own_key, shape, split, -0.22, 0.18) if split else 1.0
    result = jax.random.normal(own_key, shape, jnp.float32) * width * loudness
    return jnp.minimum(jnp.maximum(result, -limit), limit).astype(kind)


def setup_inputs(seed: int = 0) -> dict:
    keys = jax.random.split(jax.random.key(seed), 5)
    return {
        "a_band": scatter_about(keys[0], (BLOCKS, BAND, BS, BS), 0.25, 4.0, ((0, 128),)),
        "a_mask": place_ends((jax.random.randint(keys[1], (BLOCKS, BAND), 0, 8) < 5).astype(jnp.int32), jax.random.fold_in(keys[1], 1), 0, 1),
        "b_band": scatter_about(keys[2], (BLOCKS, BAND, BS, BS), 0.25, 4.0, ((0, 128),)),
        "b_mask": place_ends((jax.random.randint(keys[3], (BLOCKS, BAND), 0, 8) < 5).astype(jnp.int32), jax.random.fold_in(keys[3], 1), 0, 1),
    }


def reference(a_band, a_mask, b_band, b_mask):
    half_band = BAND // 2
    grid_rows = BLOCKS // N_ROW
    slot_count = BAND // N_COL
    col_slots = 2 * slot_count
    offsets = jnp.arange(BAND, dtype=jnp.int32)
    step_ids = jnp.arange(STEPS, dtype=jnp.int32)
    slot_ids = jnp.arange(slot_count, dtype=jnp.int32)
    out_cols = jnp.arange(N_COL * col_slots, dtype=jnp.int32)
    col_group = out_cols // col_slots
    slot_level = out_cols % col_slots

    def one_row(grid_index):
        grid_group = grid_index // grid_rows
        block_row = (grid_index % grid_rows) * N_ROW + grid_group
        left_blocks = a_band[block_row].astype(jnp.float32) * a_mask[block_row].astype(jnp.float32)[:, None, None]
        inner_rows = ((block_row + offsets - half_band) % BLOCKS).astype(jnp.int32)
        right_offs = (((half_band - grid_group - step_ids[:, None]) % N_COL) + N_COL * slot_ids[None, :]).reshape(-1).astype(jnp.int32)
        right_vals = b_band[inner_rows][:, right_offs].astype(jnp.float32)
        right_keep = b_mask[inner_rows][:, right_offs].astype(jnp.float32)
        right_blocks = right_vals * right_keep[:, :, None, None]
        products = jnp.einsum('tab,tubc->tuac', left_blocks, right_blocks, precision=lax.Precision.HIGHEST)
        target_slot = (offsets[:, None] + right_offs[None, :]).reshape(-1).astype(jnp.int32)
        band_row = jax.ops.segment_sum(products.reshape(-1, BS, BS), target_slot, num_segments=2 * BAND)
        chosen_slots = (((col_group - block_row + BAND) % N_COL) + N_COL * slot_level).astype(jnp.int32)
        return band_row[chosen_slots].astype(jnp.bfloat16)

    return lax.map(one_row, jnp.arange(BLOCKS, dtype=jnp.int32))
```

```python
import functools

import jax
import jax.numpy as jnp
from jax import lax
from jax.experimental import pallas as pl
from jax.experimental.pallas import tpu as pltpu
from jax.sharding import PartitionSpec as P

MESH = pl.DeviceIdType.MESH
BS = 128
ZORDER = (0, 1, 3, 2)


def coords():
    row, col = lax.axis_index("row"), lax.axis_index("col")
    return row // 4, row % 4, col // 4, (col // 2) % 2, col % 2


def device(x_lo, z, y, x_hi, core):
    return (x_lo * 4 + z, y * 4 + x_hi * 2 + core)


def exchange_kernel(a, b, a1, a2, a3, bs, b1, b2, sems, a1_sem, a2_sem):
    x_lo, z, y, x_hi, core = coords()
    (bs_s, bs_r, az_s, b1_s, b1_r, ax_s, b2_s, b2_r, a3_s, a3_r) = [sems.at[i] for i in range(10)]

    barrier = pltpu.get_barrier_semaphore()
    partners = [
        device(x_lo, (z + dz) % 4, y, x_hi, (core + dc) % 2)
        for dz in range(4) for dc in range(2) if (dz, dc) != (0, 0)
    ] + [
        device((x_lo + dl) % 2, z, (y + dy) % 4, (x_hi + dh) % 2, core)
        for dl in range(2) for dy in range(4) for dh in range(2) if (dl, dy, dh) != (0, 0, 0)
    ]
    for partner in partners:
        pl.semaphore_signal(barrier, inc=1, device_id=partner, device_id_type=MESH)
    pl.semaphore_wait(barrier, len(partners))

    def send(src, dst, send_sem, recv_sem, to):
        pltpu.make_async_remote_copy(
            src_ref=src, dst_ref=dst, send_sem=send_sem, recv_sem=recv_sem,
            device_id=to, device_id_type=MESH,
        ).start()

    def wait_blocks(ref, sem):
        pltpu.make_async_copy(ref, ref, sem).wait()

    sibling = device(x_lo, z, y, x_hi, 1 - core)

    send(b.at[1 - core], bs, bs_s, bs_r, sibling)

    pltpu.make_async_copy(a.at[z, pl.ds(16 * core, 16)], a1.at[z, core], a1_sem.at[0]).start()
    send(a.at[z, pl.ds(16 * (1 - core), 16)], a1.at[z, core], az_s, a1_sem.at[0], sibling)
    for g in (1, 2, 3):
        dz = ZORDER[g]
        to_z = (z + dz) % 4
        back = ZORDER.index((4 - dz) % 4)
        for part in range(4):
            for dc in range(2):
                h = (core + dc) % 2
                send(
                    a.at[to_z, pl.ds(16 * h + 4 * part, 4)],
                    a1.at[z, core, pl.ds(4 * part, 4)],
                    az_s, a1_sem.at[back],
                    device(x_lo, to_z, y, x_hi, h),
                )

    wait_blocks(bs, bs_r)
    for dc in range(2):
        cs = (core + dc) % 2
        source = b.at[core] if dc == 0 else bs
        for dl in range(2):
            to_lo = (x_lo + dl) % 2

            def pair(index, carry, cs=cs, source=source, to_lo=to_lo, dl=dl):
                q, g = index // 6, index % 6
                d = (q + core) % 2 + 2 * g
                near = d - 4 * to_lo
                col = (8 * x_hi + 4 * cs + q - d + 16) % 16
                to_y, to_hi = col // 4, (col // 2) % 2
                keep = jnp.logical_and(to_y == y, to_hi == x_hi) if dl == 0 else None
                valid = jnp.logical_and(near >= 0, near <= 6)
                slot = jnp.clip(near, 0, 6)
                dst = b1.at[slot, x_lo * 4 + y]

                def remote():
                    send(source.at[index], dst, b1_s, b1_r, device(to_lo, z, to_y, to_hi, core))

                if dl == 0:
                    @pl.when(jnp.logical_and(valid, keep))
                    def _():
                        pltpu.make_async_copy(source.at[index], dst, b1_r).start()

                    @pl.when(jnp.logical_and(valid, jnp.logical_not(keep)))
                    def _():
                        remote()
                else:
                    pl.when(valid)(remote)
                return carry

            lax.fori_loop(0, 24, pair, 0)

    def spread(g):
        zs = (z + ZORDER[g]) % 4
        wait_blocks(a1.at[zs], a1_sem.at[g])
        m = x_lo * 32 + zs * 8 + y * 2 + x_hi
        for dl in range(2):
            for dy in range(4):
                for dh in range(2):
                    to_lo, to_y, to_hi = (x_lo + dl) % 2, (y + dy) % 4, (x_hi + dh) % 2
                    to = device(to_lo, z, to_y, to_hi, core)
                    first = (4 * to_y + 2 * to_hi + 8 * x_hi) % 16

                    def put(start, at, count, to=to, to_lo=to_lo, here=(dl, dy, dh) == (0, 0, 0)):
                        src = a1.at[zs, to_lo, pl.ds(start, count)]
                        dst = a2.at[m, pl.ds(at, count)]
                        if here:
                            pltpu.make_async_copy(src, dst, a2_sem.at[g]).start()
                        else:
                            send(src, dst, ax_s, a2_sem.at[g], to)

                    @pl.when(first < 12)
                    def _():
                        put(jnp.minimum(first, 10), 0, 5)

                    @pl.when(first == 12)
                    def _():
                        put(12, 0, 4)
                        put(0, 4, 1)

                    @pl.when(first == 14)
                    def _():
                        put(14, 0, 2)
                        put(0, 2, 3)

    def share(g):
        zs = (z + ZORDER[g]) % 4
        wait_blocks(a2.at[pl.ds(0, 16)], a2_sem.at[g])
        for half in range(2):
            rows = pl.ds(half * 32 + zs * 8, 8)
            send(a2.at[rows, pl.ds(1 - core, 4)], a3.at[rows], a3_s, a3_r, sibling)

    spread(0)
    wait_blocks(b1, b1_r)
    for piece in range(4):
        for dz in (1, 3, 2):
            to_z = (z + dz) % 4
            send(b1.at[to_z + piece], b2.at[z, piece], b2_s, b2_r, device(x_lo, to_z, y, x_hi, core))
    pltpu.make_async_copy(b1.at[pl.ds(z, 4)], b2.at[z], b2_r).start()
    spread(1)
    spread(2)
    share(0)
    spread(3)
    share(1)
    share(2)
    share(3)

    wait_blocks(a3, a3_r)
    wait_blocks(b2, b2_r)
    wait_blocks(bs, bs_s)
    wait_blocks(a3, a3_s)
    wait_blocks(b2.at[pl.ds(0, 3)], b2_s)
    wait_blocks(b1, az_s)
    wait_blocks(a2.at[pl.ds(0, 60)], ax_s)
    col = 4 * y + 2 * x_hi + core
    own = 0
    for near in range(7):
        inner = (col + 4 * x_lo + near) % 16
        own = own + jnp.where(inner // 8 == x_hi, 1, 0)
    for count in range(8):
        @pl.when(own == count)
        def _(count=count):
            wait_blocks(a2.at[pl.ds(0, 56 - count), pl.ds(0, 2)], b1_s)


def exchange(a, b):
    block = (BS, BS)
    hbm = pl.BlockSpec(memory_space=pl.ANY)
    shapes = [(4, 2, 16), (64, 5), (64, 4), (24, 2), (7, 8, 2), (4, 4, 8, 2)]
    return pl.pallas_call(
        exchange_kernel,
        out_shape=[jax.ShapeDtypeStruct(shape + block, jnp.bfloat16) for shape in shapes],
        in_specs=[hbm, hbm],
        out_specs=[hbm] * len(shapes),
        scratch_shapes=[
            pltpu.SemaphoreType.DMA((10,)),
            pltpu.SemaphoreType.DMA((4,)),
            pltpu.SemaphoreType.DMA((4,)),
        ],
        compiler_params=pltpu.CompilerParams(collective_id=0, has_side_effects=True),
        name="exchange",
    )(a, b)


def product_kernel(a2, a3, b2, out, acc):
    x_lo, z, y, x_hi, core = coords()
    col = 4 * y + 2 * x_hi + core
    row = 4 * x_lo + z
    step = pl.program_id(0)
    acc[...] = jnp.zeros_like(acc)
    for odd in range(2):
        for s in range(4):
            offset = (col + s + 8 * odd) % 16
            d = row + s
            carry = jnp.where(jnp.logical_and(offset >= d, d > 0), 1, 0)
            ahead = (8 * odd + row + offset) // 16
            for other in range(2):
                h = core if other == 0 else 1 - core
                left = a2[odd, core + s] if other == 0 else a3[odd, s]
                n = (step + h - 1 + ahead + 32) % 32
                right_ref = b2.at[(n // 4) % 4, s, (n // 16) * 4 + n % 4]
                right = jnp.concatenate([right_ref[0], right_ref[1]], axis=1)
                part = jnp.dot(left, right, preferred_element_type=jnp.float32)
                at = h + carry
                acc[odd, at] += part[:, :BS]
                acc[odd, at + 1] += part[:, BS:]
    out[...] = acc[...].astype(out.dtype)


def product(a2, a3, b2):
    block = (BS, BS)
    return pl.pallas_call(
        product_kernel,
        grid=(32,),
        out_shape=jax.ShapeDtypeStruct((64, 4) + block, jnp.bfloat16),
        in_specs=[
            pl.BlockSpec((2, 5) + block, lambda i: (i, 0, 0, 0)),
            pl.BlockSpec((2, 4) + block, lambda i: (i, 0, 0, 0)),
            pl.BlockSpec(memory_space=pltpu.VMEM),
        ],
        out_specs=pl.BlockSpec((2, 4) + block, lambda i: (i, 0, 0, 0)),
        scratch_shapes=[pltpu.VMEM((2, 4) + block, jnp.float32)],
        compiler_params=pltpu.CompilerParams(vmem_limit_bytes=40 * 2**20),
        name="product",
    )(a2, a3, b2)


def local(a_band, a_mask, b_band, b_mask):
    left = a_band * a_mask[:, :, None, None].astype(jnp.bfloat16)
    right = b_band * b_mask[:, :, None, None].astype(jnp.bfloat16)
    halves = right.reshape(4, 2, 16, BS, BS)
    parities = []
    for parity in range(2):
        slots = []
        for q in range(4):
            for g in range(6):
                d = (q + parity) % 2 + 2 * g
                slots.append(halves[q, :, (16 - d) % 16])
        parities.append(jnp.stack(slots))
    right = jnp.stack(parities)
    _, a2, a3, _, _, b2 = exchange(left, right)
    return product(a2, a3, b2)


def solution(mesh):
    return jax.shard_map(
        local,
        mesh=mesh,
        in_specs=(
            P(("row", "col"), None, None, None),
            P(("row", "col"), None),
            P(("row", "col"), None, None, None),
            P(("row", "col"), None),
        ),
        out_specs=P("row", "col", None, None),
        check_vma=False,
    )
```

```python
import functools

import jax
import jax.numpy as jnp
from jax import lax
from jax.experimental import pallas as pl
from jax.experimental.pallas import tpu as pltpu
from jax.sharding import PartitionSpec as P

MESH = pl.DeviceIdType.MESH
BS = 128
ZORDER = (0, 1, 3, 2)
GROUP = 4


def coords():
    row, col = lax.axis_index("row"), lax.axis_index("col")
    return row // 4, row % 4, col // 4, (col // 2) % 2, col % 2


def device(x_lo, z, y, x_hi, core):
    return (x_lo * 4 + z, y * 4 + x_hi * 2 + core)


def exchange_kernel(a, b, left, b2, spare, a1, sa, sb, b1, sems, a1_sem, a2_sem, sa_r, b1_r):
    x_lo, z, y, x_hi, core = coords()
    x = 2 * x_hi + x_lo
    (sb_s, sb_r, sa_s, az_s, b1_s, ax_s, b2_s, b2_r, a3_s, a3_r) = [sems.at[i] for i in range(10)]

    barrier = pltpu.get_barrier_semaphore()
    partners = [device(x_lo, (z + dz) % 4, y, x_hi, core) for dz in range(1, 4)] + [
        device((x_lo + dl) % 2, z, (y + dy) % 4, (x_hi + dh) % 2, core)
        for dl in range(2) for dy in range(4) for dh in range(2) if (dl, dy, dh) != (0, 0, 0)
    ] + [device(x_lo, z, y, x_hi, 1 - core)]
    for partner in partners:
        pl.semaphore_signal(barrier, inc=1, device_id=partner, device_id_type=MESH)
    pl.semaphore_wait(barrier, len(partners))

    def send(src, dst, send_sem, recv_sem, to):
        pltpu.make_async_remote_copy(
            src_ref=src, dst_ref=dst, send_sem=send_sem, recv_sem=recv_sem,
            device_id=to, device_id_type=MESH,
        ).start()

    def wait_blocks(ref, sem):
        pltpu.make_async_copy(ref, ref, sem).wait()

    sibling = device(x_lo, z, y, x_hi, 1 - core)

    def half(q, h):
        return a.at[q, pl.ds(16 * h, 16)]

    for q in range(4):
        send(half((z + ZORDER[q]) % 4, 1 - core), sa.at[(z + ZORDER[q]) % 4], sa_s, sa_r.at[q], sibling)
    send(b.at[1 - core], sb.at[core], sb_s, sb_r, sibling)
    pltpu.make_async_copy(b.at[core], sb.at[core], sb_r).start()

    def along(g, source, cs):
        to_z = (z + ZORDER[g]) % 4
        if g == 0:
            pltpu.make_async_copy(source.at[pl.ds(0, 16)], a1.at[z, cs], a1_sem.at[0]).start()
        else:
            back = ZORDER.index((4 - ZORDER[g]) % 4)
            for part in range(4):
                at = pl.ds(4 * part, 4)
                send(source.at[at], a1.at[z, cs, at], az_s, a1_sem.at[back], device(x_lo, to_z, y, x_hi, core))

    for g in (1, 2, 3, 0):
        along(g, half((z + ZORDER[g]) % 4, core), core)
    for g in (0, 1, 2, 3):
        to_z = (z + ZORDER[g]) % 4
        wait_blocks(sa.at[to_z], sa_r.at[g])
        along(g, sa.at[to_z], 1 - core)

    wait_blocks(sb, sb_r)

    def toward(near, carry):
        for dx in range(4):
            for dy in range(4):
                to_x, to_y = (x + dx) % 4, (y + dy) % 4
                to_lo, to_hi = to_x % 2, to_x // 2
                d = near + 4 * to_lo
                inner = (4 * to_y + 2 * to_hi + core + d) % 16

                @pl.when(inner // 8 == x_hi)
                def _(dx=dx, dy=dy, to_lo=to_lo, to_y=to_y, to_hi=to_hi, d=d, inner=inner):
                    src = sb.at[(inner // 4) % 2, 6 * (inner % 4) + d // 2]
                    dst = b1.at[near, x_lo * 4 + y]
                    if (dx, dy) == (0, 0):
                        pltpu.make_async_copy(src, dst, b1_r.at[near]).start()
                    else:
                        send(src, dst, b1_s, b1_r.at[near], device(to_lo, z, to_y, to_hi, core))
        return carry

    lax.fori_loop(0, 7, toward, 0)

    def lift(near):
        wait_blocks(b1.at[near], b1_r.at[near])
        for dz in (1, 3, 2, 0):
            to_z = (z + dz) % 4
            step = near - to_z

            @pl.when(jnp.logical_and(step >= 0, step < 4))
            def _(dz=dz, to_z=to_z, step=step):
                dst = b2.at[z, jnp.clip(step, 0, 3)]
                if dz == 0:
                    pltpu.make_async_copy(b1.at[near], dst, b2_r).start()
                else:
                    send(b1.at[near], dst, b2_s, b2_r, device(x_lo, to_z, y, x_hi, core))

    def spread(g):
        zs = (z + ZORDER[g]) % 4
        wait_blocks(a1.at[zs], a1_sem.at[g])
        m = x_lo * 32 + zs * 8 + y * 2 + x_hi
        def column(index, dst):
            for dx in range(4):
                for dy in range(4):
                    to_x, to_y = (x + dx) % 4, (y + dy) % 4
                    to_lo, to_hi = to_x % 2, to_x // 2
                    src = a1.at[zs, to_lo, (4 * to_y + 2 * to_hi + index + 8 * x_hi) % 16]
                    if (dx, dy) == (0, 0):
                        pltpu.make_async_copy(src, dst, a2_sem.at[g]).start()
                    else:
                        send(src, dst, ax_s, a2_sem.at[g], device(to_lo, z, to_y, to_hi, core))

        def kept(index, carry):
            column(index + core, left.at[core, m, index])
            return carry

        column(4 * (1 - core), spare.at[m])
        lax.fori_loop(0, 4, kept, 0)

    def share(g):
        zs = (z + ZORDER[g]) % 4
        wait_blocks(left.at[0, pl.ds(0, 20)], a2_sem.at[g])
        for half in range(2):
            rows = pl.ds(half * 32 + zs * 8, 8)
            send(spare.at[rows], left.at[core, rows, 3 * (1 - core)], a3_s, a3_r, sibling)
            send(left.at[core, rows, pl.ds(1 - core, 3)], left.at[core, rows, pl.ds(core, 3)], a3_s, a3_r, sibling)

    spread(0)
    lift(0)
    lift(1)
    lift(2)
    spread(1)
    lift(3)
    lift(4)
    spread(2)
    lift(5)
    lift(6)
    share(0)
    spread(3)
    share(1)
    share(2)
    share(3)

    wait_blocks(left.at[0], a3_r)
    wait_blocks(b2, b2_r)
    wait_blocks(sb.at[0], sb_s)
    wait_blocks(sa, sa_s)
    wait_blocks(left.at[0], a3_s)
    wait_blocks(b2.at[pl.ds(0, 3)], b2_s)
    wait_blocks(left.at[0, pl.ds(0, 24)], az_s)
    wait_blocks(left.at[0, pl.ds(0, 60)], ax_s)
    wait_blocks(left.at[0, pl.ds(0, 15)], ax_s)
    col = 4 * y + 2 * x_hi + core
    own = 0
    for near in range(7):
        inner = (col + 4 * x_lo + near) % 16
        own = own + jnp.where(inner // 8 == x_hi, 1, 0)
    for count in range(8):
        @pl.when(own == count)
        def _(count=count):
            wait_blocks(left.at[0, pl.ds(0, 56 - count), pl.ds(0, 2)], b1_s)


def exchange(a, b):
    block = (BS, BS)
    hbm = pl.BlockSpec(memory_space=pl.ANY)
    shapes = [(2, 64, 4), (4, 4, 8, 2), (64,)]
    stages = [(4, 2, 16), (4, 16), (2, 24, 2), (7, 8, 2)]
    return pl.pallas_call(
        exchange_kernel,
        out_shape=[jax.ShapeDtypeStruct(shape + block, jnp.bfloat16) for shape in shapes],
        in_specs=[hbm, hbm],
        out_specs=[hbm] * len(shapes),
        scratch_shapes=[pltpu.VMEM(stage + block, jnp.bfloat16) for stage in stages] + [
            pltpu.SemaphoreType.DMA((10,)),
            pltpu.SemaphoreType.DMA((4,)),
            pltpu.SemaphoreType.DMA((4,)),
            pltpu.SemaphoreType.DMA((4,)),
            pltpu.SemaphoreType.DMA((7,)),
        ],
        compiler_params=pltpu.CompilerParams(
            collective_id=0, has_side_effects=True, vmem_limit_bytes=32 * 2**20
        ),
        name="exchange",
    )(a, b)


def product_kernel(left, b2, out, right, sems):
    x_lo, z, y, x_hi, core = coords()
    col = 4 * y + 2 * x_hi + core
    row = 4 * x_lo + z
    i = pl.program_id(0)

    def fetch(n):
        return pltpu.make_async_copy(
            b2.at[(n // 4) % 4, :, (n // 16) * 4 + n % 4], right.at[n, :, pl.ds(1, 2)], sems.at[n]
        )

    def ready(n):
        fetch(n).wait()
        for s in range(4):
            right[n, s, 0] = jnp.zeros((BS, BS), jnp.bfloat16)
            right[n, s, 3] = jnp.zeros((BS, BS), jnp.bfloat16)

    @pl.when(i == 0)
    def _():
        def begin(n, carry):
            fetch((n + 31) % 32).start()
            return carry

        lax.fori_loop(0, 32, begin, 0)
        ready(31)
        ready(0)

    for j in range(1, GROUP + 1):
        n = i * GROUP + j
        pl.when(n < 31)(functools.partial(ready, n))

    for odd in range(2):
        before = None
        for j in range(-1, GROUP):
            weights = []
            for s in range(4):
                offset = (col + s + 8 * odd) % 16
                d = row + s
                first = jnp.where(jnp.logical_and(offset >= d, d > 0), 0, 1)
                n = (i * GROUP + j + (8 * odd + row + offset) // 16 + 32) % 32
                weights.append(jnp.concatenate([right[n, s, first + l] for l in range(3)], axis=1))
            lines = []
            if j >= 0:
                lines.append(jnp.concatenate([left[1, 2 * j + odd, s] for s in range(4)], axis=1))
            if j < GROUP - 1:
                lines.append(jnp.concatenate([left[0, 2 * j + 2 + odd, s] for s in range(4)], axis=1))
            part = jnp.dot(
                jnp.concatenate(lines, axis=0), jnp.concatenate(weights, axis=0), preferred_element_type=jnp.float32
            )
            if j >= 0:
                here = part[:BS]
                sums = [
                    before[:, :BS],
                    before[:, BS:2 * BS] + here[:, :BS],
                    before[:, 2 * BS:] + here[:, BS:2 * BS],
                    here[:, 2 * BS:],
                ]
                for l in range(4):
                    out[2 * j + odd, l] = sums[l].astype(out.dtype)
            before = part[-BS:]


def product(left, b2):
    block = (BS, BS)
    return pl.pallas_call(
        product_kernel,
        grid=(32 // GROUP,),
        out_shape=jax.ShapeDtypeStruct((64, 4) + block, jnp.bfloat16),
        in_specs=[
            pl.BlockSpec((2, 2 * GROUP, 4) + block, lambda i: (0, i, 0, 0, 0)),
            pl.BlockSpec(memory_space=pl.ANY),
        ],
        out_specs=pl.BlockSpec((2 * GROUP, 4) + block, lambda i: (i, 0, 0, 0)),
        scratch_shapes=[pltpu.VMEM((32, 4, 4) + block, jnp.bfloat16), pltpu.SemaphoreType.DMA((32,))],
        compiler_params=pltpu.CompilerParams(vmem_limit_bytes=48 * 2**20),
        name="product",
    )(left, b2)


def local(a_band, a_mask, b_band, b_mask):
    left = a_band * a_mask[:, :, None, None].astype(jnp.bfloat16)
    right = b_band * b_mask[:, :, None, None].astype(jnp.bfloat16)
    halves = right.reshape(4, 2, 16, BS, BS)
    parities = []
    for parity in range(2):
        slots = []
        for q in range(4):
            for g in range(6):
                d = (q + parity) % 2 + 2 * g
                slots.append(halves[q, :, (16 - d) % 16])
        parities.append(jnp.stack(slots))
    right = jnp.stack(parities)
    left, right, _ = exchange(left, right)
    return product(left, right)


def solution(mesh):
    return jax.shard_map(
        local,
        mesh=mesh,
        in_specs=(
            P(("row", "col"), None, None, None),
            P(("row", "col"), None),
            P(("row", "col"), None, None, None),
            P(("row", "col"), None),
        ),
        out_specs=P("row", "col", None, None),
        check_vma=False,
    )
```

```python
import functools

import jax
import jax.numpy as jnp
from jax import lax
from jax.experimental import pallas as pl
from jax.experimental.pallas import tpu as pltpu
from jax.sharding import PartitionSpec as P

MESH = pl.DeviceIdType.MESH
BS = 128
ZORDER = (0, 1, 3, 2)
GROUP = 8
EXCHANGE_VMEM = 58 * 2**20
PRODUCT_VMEM = 58 * 2**20


def coords():
    row, col = lax.axis_index("row"), lax.axis_index("col")
    return row // 4, row % 4, col // 4, (col // 2) % 2, col % 2


def device(x_lo, z, y, x_hi, core):
    return (x_lo * 4 + z, y * 4 + x_hi * 2 + core)


def exchange_kernel(
    a, am, b, bm, left, b2, ar, br, a1, sa, bp, b1, spare, sems, load_sem, a1_sem, sa_r, b1_r, a2_sem
):
    x_lo, z, y, x_hi, core = coords()
    x = 2 * x_hi + x_lo
    (bp_s, bp_r, sa_s, az_s, b1_s, ax_s, b2_s, b2_r, a3_s, a3_r) = [sems.at[i] for i in range(10)]

    def send(src, dst, send_sem, recv_sem, to):
        pltpu.make_async_remote_copy(
            src_ref=src, dst_ref=dst, send_sem=send_sem, recv_sem=recv_sem,
            device_id=to, device_id_type=MESH,
        ).start()

    def wait_blocks(ref, sem):
        pltpu.make_async_copy(ref, ref, sem).wait()

    def load(g, h):
        q = (z + ZORDER[g]) % 4
        return pltpu.make_async_copy(a.at[q, pl.ds(16 * h, 16)], ar.at[q, h], load_sem.at[2 * g + (h + core) % 2])

    def load_b(q):
        return pltpu.make_async_copy(b.at[q], br.at[q], load_sem.at[8 + q])

    for q in range(4):
        load_b(q).start()
    for h in (1 - core, core):
        for g in range(4):
            load(g, h).start()

    barrier = pltpu.get_barrier_semaphore()
    sibling = device(x_lo, z, y, x_hi, 1 - core)
    partners = [device(x_lo, (z + dz) % 4, y, x_hi, core) for dz in range(1, 4)] + [
        device((x + dx) % 4 % 2, z, (y + dy) % 4, (x + dx) % 4 // 2, core)
        for dx in range(4) for dy in range(4) if (dx, dy) != (0, 0)
    ] + [sibling]
    for partner in partners:
        pl.semaphore_signal(barrier, inc=1, device_id=partner, device_id_type=MESH)

    for q in range(4):
        load_b(q).wait()

    def mask_b(q, carry):
        for d in range(11):
            for h in range(2):
                u = (16 - d) % 16
                keep = bm[q, 16 * h + u].astype(jnp.float32)
                bp[(q + d) % 2, 6 * q + d // 2, h] = (br[q, 16 * h + u].astype(jnp.float32) * keep).astype(jnp.bfloat16)
        bp[(q + 1) % 2, 6 * q + 5] = jnp.zeros((2, BS, BS), jnp.bfloat16)
        return carry

    lax.fori_loop(0, 4, mask_b, 0)
    pl.semaphore_wait(barrier, len(partners))
    send(bp.at[1 - core], bp.at[2], bp_s, bp_r, sibling)

    def mask_a(g, h):
        q = (z + ZORDER[g]) % 4
        load(g, h).wait()

        def one(t, carry):
            keep = am[q, 16 * h + t].astype(jnp.float32)
            ar[q, h, t] = (ar[q, h, t].astype(jnp.float32) * keep).astype(jnp.bfloat16)
            return carry

        lax.fori_loop(0, 16, one, 0)

    for g in range(4):
        mask_a(g, 1 - core)
        q = (z + ZORDER[g]) % 4
        send(ar.at[q, 1 - core], sa.at[q], sa_s, sa_r.at[g], sibling)

    def toward(near, carry, mine):
        for dx in range(4):
            for dy in range(4):
                to_x, to_y = (x + dx) % 4, (y + dy) % 4
                to_lo, to_hi = to_x % 2, to_x // 2
                d = near + 4 * to_lo
                inner = (4 * to_y + 2 * to_hi + core + d) % 16
                wanted = 2 * x_hi + (core if mine else 1 - core)

                @pl.when(inner // 4 == wanted)
                def _(dx=dx, dy=dy, to_lo=to_lo, to_y=to_y, to_hi=to_hi, d=d, inner=inner):
                    src = bp.at[core if mine else 2, 6 * (inner % 4) + d // 2]
                    dst = b1.at[near, x_lo * 4 + y]
                    if (dx, dy) == (0, 0):
                        pltpu.make_async_copy(src, dst, b1_r.at[near]).start()
                    else:
                        send(src, dst, b1_s, b1_r.at[near], device(to_lo, z, to_y, to_hi, core))
        return carry

    lax.fori_loop(0, 7, functools.partial(toward, mine=True), 0)

    def along(g, source, cs):
        to_z = (z + ZORDER[g]) % 4
        if g == 0:
            pltpu.make_async_copy(source, a1.at[z, cs], a1_sem.at[0]).start()
        else:
            back = ZORDER.index((4 - ZORDER[g]) % 4)
            for part in range(4):
                at = pl.ds(4 * part, 4)
                send(source.at[at], a1.at[z, cs, at], az_s, a1_sem.at[back], device(x_lo, to_z, y, x_hi, core))

    for g in (1, 2, 3, 0):
        mask_a(g, core)
        along(g, ar.at[(z + ZORDER[g]) % 4, core], core)
    for g in (0, 1, 2, 3):
        to_z = (z + ZORDER[g]) % 4
        wait_blocks(sa.at[to_z], sa_r.at[g])
        along(g, sa.at[to_z], 1 - core)

    wait_blocks(bp.at[2], bp_r)
    lax.fori_loop(0, 7, functools.partial(toward, mine=False), 0)

    def lift(near):
        wait_blocks(b1.at[near], b1_r.at[near])
        for dz in (1, 3, 2, 0):
            to_z = (z + dz) % 4
            step = near - to_z

            @pl.when(jnp.logical_and(step >= 0, step < 4))
            def _(dz=dz, to_z=to_z, step=step):
                dst = b2.at[z, jnp.clip(step, 0, 3)]
                if dz == 0:
                    pltpu.make_async_copy(b1.at[near], dst, b2_r).start()
                else:
                    send(b1.at[near], dst, b2_s, b2_r, device(x_lo, to_z, y, x_hi, core))

    def spread(g):
        zs = (z + ZORDER[g]) % 4
        wait_blocks(a1.at[zs], a1_sem.at[g])
        m = x_lo * 32 + zs * 8 + y * 2 + x_hi

        def column(index, dst, sem):
            for dx in range(4):
                for dy in range(4):
                    to_x, to_y = (x + dx) % 4, (y + dy) % 4
                    to_lo, to_hi = to_x % 2, to_x // 2
                    src = a1.at[zs, to_lo, (4 * to_y + 2 * to_hi + index + 8 * x_hi) % 16]
                    if (dx, dy) == (0, 0):
                        pltpu.make_async_copy(src, dst, sem).start()
                    else:
                        send(src, dst, ax_s, sem, device(to_lo, z, to_y, to_hi, core))

        def both(index, carry):
            column(index, left.at[core, m, index - core], a2_sem.at[g, index])
            return carry

        column(4 * (1 - core), spare.at[m], a2_sem.at[g, 0])
        lax.fori_loop(1, 4, both, 0)
        column(4 * core, left.at[core, m, 3 * core], a2_sem.at[g, 4])

    def share(g):
        zs = (z + ZORDER[g]) % 4
        for index in range(4):
            wait_blocks(spare.at[pl.ds(0, 16)], a2_sem.at[g, index])
            for half in range(2):
                rows = pl.ds(half * 32 + zs * 8, 8)
                if index == 0:
                    send(spare.at[rows], left.at[core, rows, 3 * (1 - core)], a3_s, a3_r, sibling)
                else:
                    send(
                        left.at[core, rows, index - core], left.at[core, rows, index - 1 + core],
                        a3_s, a3_r, sibling,
                    )

    spread(0)
    lift(0)
    lift(1)
    lift(2)
    spread(1)
    lift(3)
    lift(4)
    spread(2)
    lift(5)
    lift(6)
    share(0)
    spread(3)
    share(1)
    share(2)
    share(3)

    for g in range(4):
        wait_blocks(spare.at[pl.ds(0, 16)], a2_sem.at[g, 4])
    wait_blocks(left.at[0], a3_r)
    wait_blocks(b2, b2_r)
    wait_blocks(bp.at[0], bp_s)
    wait_blocks(sa, sa_s)
    wait_blocks(left.at[0], a3_s)
    wait_blocks(b2.at[pl.ds(0, 3)], b2_s)
    wait_blocks(left.at[0, pl.ds(0, 24)], az_s)
    wait_blocks(left.at[:, pl.ds(0, 50), pl.ds(0, 3)], ax_s)
    col = 4 * y + 2 * x_hi + core
    own = 0
    for near in range(7):
        inner = (col + 4 * x_lo + near) % 16
        own = own + jnp.where(inner // 8 == x_hi, 1, 0)
    for count in range(8):
        @pl.when(own == count)
        def _(count=count):
            wait_blocks(left.at[0, pl.ds(0, 56 - count), pl.ds(0, 2)], b1_s)


def exchange(a, am, b, bm):
    block = (BS, BS)
    hbm = pl.BlockSpec(memory_space=pl.ANY)
    smem = pl.BlockSpec(memory_space=pltpu.SMEM)
    shapes = [(2, 64, 4), (4, 4, 8, 2)]
    stages = [(4, 2, 16), (4, 32), (4, 2, 16), (4, 16), (3, 24, 2), (7, 8, 2), (64,)]
    semaphores = [(10,), (12,), (4,), (4,), (7,), (4, 5)]
    return pl.pallas_call(
        exchange_kernel,
        out_shape=[jax.ShapeDtypeStruct(shape + block, jnp.bfloat16) for shape in shapes],
        in_specs=[hbm, smem, hbm, smem],
        out_specs=[hbm] * len(shapes),
        scratch_shapes=[pltpu.VMEM(stage + block, jnp.bfloat16) for stage in stages]
        + [pltpu.SemaphoreType.DMA(shape) for shape in semaphores],
        compiler_params=pltpu.CompilerParams(
            collective_id=0, has_side_effects=True, vmem_limit_bytes=EXCHANGE_VMEM
        ),
        name="exchange",
    )(a, am, b, bm)


def product_kernel(left, b2, out, right, sems):
    x_lo, z, y, x_hi, core = coords()
    col = 4 * y + 2 * x_hi + core
    row = 4 * x_lo + z
    i = pl.program_id(0)

    def fetch(n):
        return pltpu.make_async_copy(
            b2.at[(n // 4) % 4, :, (n // 16) * 4 + n % 4], right.at[n, :, pl.ds(1, 2)], sems.at[n]
        )

    def ready(n):
        fetch(n).wait()
        for s in range(4):
            right[n, s, 0] = jnp.zeros((BS, BS), jnp.bfloat16)
            right[n, s, 3] = jnp.zeros((BS, BS), jnp.bfloat16)

    @pl.when(i == 0)
    def _():
        def begin(n, carry):
            fetch((n + 31) % 32).start()
            return carry

        lax.fori_loop(0, 32, begin, 0)
        ready(31)
        ready(0)

    for j in range(1, GROUP + 1):
        n = i * GROUP + j
        pl.when(n < 31)(functools.partial(ready, n))

    for odd in range(2):
        before = None
        for j in range(-1, GROUP):
            weights = []
            for s in range(4):
                offset = (col + s + 8 * odd) % 16
                d = row + s
                first = jnp.where(jnp.logical_and(offset >= d, d > 0), 0, 1)
                n = (i * GROUP + j + (8 * odd + row + offset) // 16 + 32) % 32
                weights.append(jnp.concatenate([right[n, s, first + l] for l in range(3)], axis=1))
            lines = []
            if j >= 0:
                lines.append(jnp.concatenate([left[1, 2 * j + odd, s] for s in range(4)], axis=1))
            if j < GROUP - 1:
                lines.append(jnp.concatenate([left[0, 2 * j + 2 + odd, s] for s in range(4)], axis=1))
            part = jnp.dot(
                jnp.concatenate(lines, axis=0), jnp.concatenate(weights, axis=0), preferred_element_type=jnp.float32
            )
            if j >= 0:
                here = part[:BS]
                sums = [
                    before[:, :BS],
                    before[:, BS:2 * BS] + here[:, :BS],
                    before[:, 2 * BS:] + here[:, BS:2 * BS],
                    here[:, 2 * BS:],
                ]
                for l in range(4):
                    out[2 * j + odd, l] = sums[l].astype(out.dtype)
            before = part[-BS:]


def product(left, b2):
    block = (BS, BS)
    return pl.pallas_call(
        product_kernel,
        grid=(32 // GROUP,),
        out_shape=jax.ShapeDtypeStruct((64, 4) + block, jnp.bfloat16),
        in_specs=[
            pl.BlockSpec((2, 2 * GROUP, 4) + block, lambda i: (0, i, 0, 0, 0)),
            pl.BlockSpec(memory_space=pl.ANY),
        ],
        out_specs=pl.BlockSpec((2 * GROUP, 4) + block, lambda i: (i, 0, 0, 0)),
        scratch_shapes=[pltpu.VMEM((32, 4, 4) + block, jnp.bfloat16), pltpu.SemaphoreType.DMA((32,))],
        compiler_params=pltpu.CompilerParams(vmem_limit_bytes=PRODUCT_VMEM),
        name="product",
    )(left, b2)


def local(a_band, a_mask, b_band, b_mask):
    left, right = exchange(a_band, a_mask, b_band, b_mask)
    return product(left, right)


def solution(mesh):
    return jax.shard_map(
        local,
        mesh=mesh,
        in_specs=(
            P(("row", "col"), None, None, None),
            P(("row", "col"), None),
            P(("row", "col"), None, None, None),
            P(("row", "col"), None),
        ),
        out_specs=P("row", "col", None, None),
        check_vma=False,
    )
```

```python
import functools

import jax
import jax.numpy as jnp
from jax import lax
from jax.experimental import pallas as pl
from jax.experimental.pallas import tpu as pltpu
from jax.sharding import PartitionSpec as P

MESH = pl.DeviceIdType.MESH
BS = 128
ZORDER = (0, 1, 3, 2)
GROUP = 8
EXCHANGE_VMEM = 58 * 2**20
PRODUCT_VMEM = 58 * 2**20


def coords():
    row, col = lax.axis_index("row"), lax.axis_index("col")
    return row // 4, row % 4, col // 4, (col // 2) % 2, col % 2


def device(x_lo, z, y, x_hi, core):
    return (x_lo * 4 + z, y * 4 + x_hi * 2 + core)


def exchange_kernel(
    a, am, b, bm, left, b2, ar, br, a1, ay, sa, bp, b1, spare,
    sems, load_sem, a1_sem, ay_r, sa_r, b1_r, a2_sem
):
    x_lo, z, y, x_hi, core = coords()
    x = 2 * x_hi + x_lo
    (bp_s, bp_r, sa_s, az_s, b1_s, ax_s, b2_s, b2_r, a3_s, a3_r, ay_s, relay_s) = [
        sems.at[i] for i in range(12)
    ]

    def send(src, dst, send_sem, recv_sem, to):
        pltpu.make_async_remote_copy(
            src_ref=src, dst_ref=dst, send_sem=send_sem, recv_sem=recv_sem,
            device_id=to, device_id_type=MESH,
        ).start()

    def wait_blocks(ref, sem):
        pltpu.make_async_copy(ref, ref, sem).wait()

    def load(g, h):
        q = (z + ZORDER[g]) % 4
        return pltpu.make_async_copy(a.at[q, pl.ds(16 * h, 16)], ar.at[q, h], load_sem.at[2 * g + (h + core) % 2])

    def load_b(q):
        return pltpu.make_async_copy(b.at[q], br.at[q], load_sem.at[8 + q])

    for q in range(4):
        load_b(q).start()
    for h in (1 - core, core):
        for g in range(4):
            load(g, h).start()

    barrier = pltpu.get_barrier_semaphore()
    sibling = device(x_lo, z, y, x_hi, 1 - core)
    partners = [device(x_lo, (z + dz) % 4, y, x_hi, core) for dz in range(1, 4)] + [
        device((x + dx) % 4 % 2, z, (y + dy) % 4, (x + dx) % 4 // 2, core)
        for dx in range(4) for dy in range(4) if (dx, dy) != (0, 0)
    ] + [sibling]
    for partner in partners:
        pl.semaphore_signal(barrier, inc=1, device_id=partner, device_id_type=MESH)

    for q in range(4):
        load_b(q).wait()

    def mask_b(q, carry):
        for d in range(11):
            for h in range(2):
                u = (16 - d) % 16
                keep = bm[q, 16 * h + u].astype(jnp.float32)
                bp[(q + d) % 2, 6 * q + d // 2, h] = (br[q, 16 * h + u].astype(jnp.float32) * keep).astype(jnp.bfloat16)
        bp[(q + 1) % 2, 6 * q + 5] = jnp.zeros((2, BS, BS), jnp.bfloat16)
        return carry

    lax.fori_loop(0, 4, mask_b, 0)
    pl.semaphore_wait(barrier, len(partners))
    send(bp.at[1 - core], bp.at[2], bp_s, bp_r, sibling)

    def mask_a(g, h):
        q = (z + ZORDER[g]) % 4
        load(g, h).wait()

        def one(t, carry):
            keep = am[q, 16 * h + t].astype(jnp.float32)
            ar[q, h, t] = (ar[q, h, t].astype(jnp.float32) * keep).astype(jnp.bfloat16)
            return carry

        lax.fori_loop(0, 16, one, 0)

    for g in range(4):
        mask_a(g, 1 - core)
        q = (z + ZORDER[g]) % 4
        send(ar.at[q, 1 - core], sa.at[q], sa_s, sa_r.at[g], sibling)

    def toward(near, carry, mine):
        for dx in range(4):
            for dy in range(4):
                to_x, to_y = (x + dx) % 4, (y + dy) % 4
                to_lo, to_hi = to_x % 2, to_x // 2
                d = near + 4 * to_lo
                inner = (4 * to_y + 2 * to_hi + core + d) % 16
                wanted = 2 * x_hi + (core if mine else 1 - core)

                @pl.when(inner // 4 == wanted)
                def _(dx=dx, dy=dy, to_lo=to_lo, to_y=to_y, to_hi=to_hi, d=d, inner=inner):
                    src = bp.at[core if mine else 2, 6 * (inner % 4) + d // 2]
                    dst = b1.at[near, x_lo * 4 + y]
                    if (dx, dy) == (0, 0):
                        pltpu.make_async_copy(src, dst, b1_r.at[near]).start()
                    else:
                        send(src, dst, b1_s, b1_r.at[near], device(to_lo, z, to_y, to_hi, core))
        return carry

    lax.fori_loop(0, 7, functools.partial(toward, mine=True), 0)

    def along(g, source, cs):
        to_z = (z + ZORDER[g]) % 4
        if g == 0:
            pltpu.make_async_copy(source, a1.at[z, cs], a1_sem.at[0]).start()
        else:
            back = ZORDER.index((4 - ZORDER[g]) % 4)
            for part in range(4):
                at = pl.ds(4 * part, 4)
                send(source.at[at], a1.at[z, cs, at], az_s, a1_sem.at[back], device(x_lo, to_z, y, x_hi, core))

    for g in (1, 2, 3, 0):
        mask_a(g, core)
        along(g, ar.at[(z + ZORDER[g]) % 4, core], core)
    for g in (0, 1, 2, 3):
        to_z = (z + ZORDER[g]) % 4
        wait_blocks(sa.at[to_z], sa_r.at[g])
        along(g, sa.at[to_z], 1 - core)

    wait_blocks(bp.at[2], bp_r)
    lax.fori_loop(0, 7, functools.partial(toward, mine=False), 0)

    def lift(near):
        wait_blocks(b1.at[near], b1_r.at[near])
        for dz in (1, 3, 2, 0):
            to_z = (z + dz) % 4
            step = near - to_z

            @pl.when(jnp.logical_and(step >= 0, step < 4))
            def _(dz=dz, to_z=to_z, step=step):
                dst = b2.at[z, jnp.clip(step, 0, 3)]
                if dz == 0:
                    pltpu.make_async_copy(b1.at[near], dst, b2_r).start()
                else:
                    send(b1.at[near], dst, b2_s, b2_r, device(x_lo, to_z, y, x_hi, core))

    def rows_from(zs, half):
        return pl.ds(half * 32 + zs * 8, 8)

    def land(index, m, src, sem, to):
        def put(dst):
            if to is None:
                pltpu.make_async_copy(src, dst, sem).start()
            else:
                send(src, dst, ax_s, sem, to)

        @pl.when(index == 4 * (1 - core))
        def _():
            put(spare.at[m])

        @pl.when(index != 4 * (1 - core))
        def _():
            put(left.at[core, m, jnp.clip(index - core, 0, 3)])

    def outer_sem(index, half):
        return jnp.where(jnp.logical_and(half == 1, index % 4 == 0), 5 + index // 4, index)

    def along_y(g):
        zs = (z + ZORDER[g]) % 4
        wait_blocks(a1.at[zs], a1_sem.at[g])
        for k in range(3):
            for cs in range(2):
                for dy in (1, 3, 2, 0):
                    to_y = (y + dy) % 4
                    src = a1.at[zs, cs, (4 * to_y + 2 + k + 8 * x_hi) % 16]
                    dst = ay.at[zs, y, cs, k]
                    if dy == 0:
                        pltpu.make_async_copy(src, dst, ay_r.at[g]).start()
                    else:
                        send(src, dst, ay_s, ay_r.at[g], device(x_lo, z, to_y, x_hi, core))

    def along_x(g):
        zs = (z + ZORDER[g]) % 4
        wait_blocks(ay.at[zs], ay_r.at[g])

        def one(from_y, carry):
            m = x_lo * 32 + zs * 8 + from_y * 2 + x_hi
            for k in (0, 2, 1):
                for dx in (1, 3, 2, 0):
                    to_x = (x + dx) % 4
                    to_lo, to_hi = to_x % 2, to_x // 2
                    index = k + 2 * (1 - to_hi)
                    to = None if dx == 0 else device(to_lo, z, y, to_hi, core)
                    src = ay.at[zs, from_y, to_lo, k]
                    if k == 1:
                        land(index, m, src, a2_sem.at[g, index], to)
                    else:
                        relayed = jnp.logical_and(x_lo == 1, to_hi == (0 if k == 2 else 1))

                        @pl.when(jnp.logical_not(relayed))
                        def _(index=index, src=src, to=to):
                            land(index, m, src, a2_sem.at[g, outer_sem(index, x_lo)], to)
            return carry

        lax.fori_loop(0, 4, one, 0)

    def direct(g):
        zs = (z + ZORDER[g]) % 4
        m = x_lo * 32 + zs * 8 + y * 2 + x_hi

        def column(outer):
            for dx in range(4):
                for dy in range(4):
                    to_x, to_y = (x + dx) % 4, (y + dy) % 4
                    to_lo, to_hi = to_x % 2, to_x // 2
                    index = 4 * to_hi if outer else 1 + 2 * to_hi
                    src = a1.at[zs, to_lo, (4 * to_y + 2 * to_hi + index + 8 * x_hi) % 16]
                    to = None if (dx, dy) == (0, 0) else device(to_lo, z, to_y, to_hi, core)
                    land(index, m, src, a2_sem.at[g, outer_sem(index, x_lo)], to)

        column(False)

        @pl.when(x_lo == 1)
        def _():
            column(True)

    def relay(g):
        zs = (z + ZORDER[g]) % 4
        for half in range(2):
            side = (x_hi + half) % 2
            wait_blocks(spare.at[pl.ds(0, 8)], a2_sem.at[g, outer_sem(4 * (1 - side), half)])
            to = device(x_lo, z, (y + 1 + 2 * side) % 4, x_hi, core)
            sem = a2_sem.at[g, outer_sem(4 * side, half)]
            rows = rows_from(zs, half)
            mine, other = left.at[core, rows, 3 * core], spare.at[rows]

            @pl.when(core == side)
            def _(mine=mine, other=other, sem=sem, to=to):
                send(other, mine, relay_s, sem, to)

            @pl.when(core != side)
            def _(mine=mine, other=other, sem=sem, to=to):
                send(mine, other, relay_s, sem, to)

    def share(g):
        zs = (z + ZORDER[g]) % 4
        for index in (2, 1, 3, 0):
            if index == 0:
                for half in range(2):
                    side = (x_hi + half) % 2
                    wait_blocks(spare.at[pl.ds(0, 8)], a2_sem.at[g, outer_sem(4 * side, half)])
            else:
                wait_blocks(spare.at[pl.ds(0, 16)], a2_sem.at[g, index])
            for half in range(2):
                rows = rows_from(zs, half)
                if index == 0:
                    send(spare.at[rows], left.at[core, rows, 3 * (1 - core)], a3_s, a3_r, sibling)
                else:
                    send(
                        left.at[core, rows, index - core], left.at[core, rows, index - 1 + core],
                        a3_s, a3_r, sibling,
                    )

    along_y(0)
    along_x(0)
    lift(0)
    lift(1)
    lift(2)
    lift(3)
    lift(4)
    along_y(1)
    along_y(2)
    lift(5)
    lift(6)
    along_y(3)
    along_x(1)
    direct(0)
    direct(1)
    along_x(2)
    direct(2)
    direct(3)
    relay(0)
    share(0)
    along_x(3)
    relay(1)
    share(1)
    relay(2)
    share(2)
    relay(3)
    share(3)

    wait_blocks(left.at[0], a3_r)
    wait_blocks(b2, b2_r)
    wait_blocks(bp.at[0], bp_s)
    wait_blocks(sa, sa_s)
    wait_blocks(left.at[0], a3_s)
    wait_blocks(b2.at[pl.ds(0, 3)], b2_s)
    wait_blocks(left.at[0, pl.ds(0, 24)], az_s)
    wait_blocks(left.at[0, pl.ds(0, 18)], ay_s)
    for half, count in ((0, 51), (1, 54)):
        @pl.when(x_lo == half)
        def _(count=count):
            wait_blocks(left.at[0, pl.ds(0, count)], ax_s)

    wait_blocks(spare, relay_s)
    col = 4 * y + 2 * x_hi + core
    own = 0
    for near in range(7):
        inner = (col + 4 * x_lo + near) % 16
        own = own + jnp.where(inner // 8 == x_hi, 1, 0)
    for count in range(8):
        @pl.when(own == count)
        def _(count=count):
            wait_blocks(left.at[0, pl.ds(0, 56 - count), pl.ds(0, 2)], b1_s)


def exchange(a, am, b, bm):
    block = (BS, BS)
    hbm = pl.BlockSpec(memory_space=pl.ANY)
    smem = pl.BlockSpec(memory_space=pltpu.SMEM)
    shapes = [(2, 64, 4), (4, 4, 8, 2)]
    stages = [(4, 2, 16), (4, 32), (4, 2, 16), (4, 4, 2, 3), (4, 16), (3, 24, 2), (7, 8, 2), (64,)]
    semaphores = [(12,), (12,), (4,), (4,), (4,), (7,), (4, 7)]
    return pl.pallas_call(
        exchange_kernel,
        out_shape=[jax.ShapeDtypeStruct(shape + block, jnp.bfloat16) for shape in shapes],
        in_specs=[hbm, smem, hbm, smem],
        out_specs=[hbm] * len(shapes),
        scratch_shapes=[pltpu.VMEM(stage + block, jnp.bfloat16) for stage in stages]
        + [pltpu.SemaphoreType.DMA(shape) for shape in semaphores],
        compiler_params=pltpu.CompilerParams(
            collective_id=0, has_side_effects=True, vmem_limit_bytes=EXCHANGE_VMEM
        ),
        name="exchange",
    )(a, am, b, bm)


def product_kernel(left, b2, out, right, sems):
    x_lo, z, y, x_hi, core = coords()
    col = 4 * y + 2 * x_hi + core
    row = 4 * x_lo + z
    i = pl.program_id(0)

    def fetch(n):
        return pltpu.make_async_copy(
            b2.at[(n // 4) % 4, :, (n // 16) * 4 + n % 4], right.at[n, :, pl.ds(1, 2)], sems.at[n]
        )

    def ready(n):
        fetch(n).wait()
        for s in range(4):
            right[n, s, 0] = jnp.zeros((BS, BS), jnp.bfloat16)
            right[n, s, 3] = jnp.zeros((BS, BS), jnp.bfloat16)

    @pl.when(i == 0)
    def _():
        def begin(n, carry):
            fetch((n + 31) % 32).start()
            return carry

        lax.fori_loop(0, 32, begin, 0)
        ready(31)
        ready(0)

    for j in range(1, GROUP + 1):
        n = i * GROUP + j
        pl.when(n < 31)(functools.partial(ready, n))

    for odd in range(2):
        before = None
        for j in range(-1, GROUP):
            weights = []
            for s in range(4):
                offset = (col + s + 8 * odd) % 16
                d = row + s
                first = jnp.where(jnp.logical_and(offset >= d, d > 0), 0, 1)
                n = (i * GROUP + j + (8 * odd + row + offset) // 16 + 32) % 32
                weights.append(jnp.concatenate([right[n, s, first + l] for l in range(3)], axis=1))
            lines = []
            if j >= 0:
                lines.append(jnp.concatenate([left[1, 2 * j + odd, s] for s in range(4)], axis=1))
            if j < GROUP - 1:
                lines.append(jnp.concatenate([left[0, 2 * j + 2 + odd, s] for s in range(4)], axis=1))
            part = jnp.dot(
                jnp.concatenate(lines, axis=0), jnp.concatenate(weights, axis=0), preferred_element_type=jnp.float32
            )
            if j >= 0:
                here = part[:BS]
                sums = [
                    before[:, :BS],
                    before[:, BS:2 * BS] + here[:, :BS],
                    before[:, 2 * BS:] + here[:, BS:2 * BS],
                    here[:, 2 * BS:],
                ]
                for l in range(4):
                    out[2 * j + odd, l] = sums[l].astype(out.dtype)
            before = part[-BS:]


def product(left, b2):
    block = (BS, BS)
    return pl.pallas_call(
        product_kernel,
        grid=(32 // GROUP,),
        out_shape=jax.ShapeDtypeStruct((64, 4) + block, jnp.bfloat16),
        in_specs=[
            pl.BlockSpec((2, 2 * GROUP, 4) + block, lambda i: (0, i, 0, 0, 0)),
            pl.BlockSpec(memory_space=pl.ANY),
        ],
        out_specs=pl.BlockSpec((2 * GROUP, 4) + block, lambda i: (i, 0, 0, 0)),
        scratch_shapes=[pltpu.VMEM((32, 4, 4) + block, jnp.bfloat16), pltpu.SemaphoreType.DMA((32,))],
        compiler_params=pltpu.CompilerParams(vmem_limit_bytes=PRODUCT_VMEM),
        name="product",
    )(left, b2)


def local(a_band, a_mask, b_band, b_mask):
    left, right = exchange(a_band, a_mask, b_band, b_mask)
    return product(left, right)


def solution(mesh):
    return jax.shard_map(
        local,
        mesh=mesh,
        in_specs=(
            P(("row", "col"), None, None, None),
            P(("row", "col"), None),
            P(("row", "col"), None, None, None),
            P(("row", "col"), None),
        ),
        out_specs=P("row", "col", None, None),
        check_vma=False,
    )
```

```python
import functools

import jax
import jax.numpy as jnp
from jax import lax
from jax.experimental import pallas as pl
from jax.experimental.pallas import tpu as pltpu
from jax.sharding import PartitionSpec as P

MESH = pl.DeviceIdType.MESH
BS = 128
ZORDER = (0, 1, 3, 2)
VMEM = 58 * 2**20


def coords():
    row, col = lax.axis_index("row"), lax.axis_index("col")
    return row // 4, row % 4, col // 4, (col // 2) % 2, col % 2


def device(x_lo, z, y, x_hi, core):
    return (x_lo * 4 + z, y * 4 + x_hi * 2 + core)


def product_kernel(
    a, am, b, bm, out, left, b2, ar, br, a1, ay, sa, bp, b1, spare,
    sems, load_sem, a1_sem, ay_r, sa_r, b1_r, a2_sem, near_r, a3_r, out_sem
):
    x_lo, z, y, x_hi, core = coords()
    x = 2 * x_hi + x_lo
    (bp_s, bp_r, sa_s, az_s, b1_s, ax_s, b2_s, b2_r, a3_s, ay_s, relay_s, far_s) = [
        sems.at[i] for i in range(12)
    ]

    def send(src, dst, send_sem, recv_sem, to):
        pltpu.make_async_remote_copy(
            src_ref=src, dst_ref=dst, send_sem=send_sem, recv_sem=recv_sem,
            device_id=to, device_id_type=MESH,
        ).start()

    def wait_blocks(ref, sem):
        pltpu.make_async_copy(ref, ref, sem).wait()

    def masked(block, keep):
        factor = jnp.full((16, BS), keep.astype(jnp.float32)).astype(jnp.bfloat16)
        return (block.reshape(BS // 16, 16, BS) * factor[None]).reshape(BS, BS)

    def load(g, h):
        q = (z + ZORDER[g]) % 4
        return pltpu.make_async_copy(a.at[q, pl.ds(16 * h, 16)], ar.at[q, h], load_sem.at[2 * g + (h + core) % 2])

    def load_b(q):
        return pltpu.make_async_copy(b.at[q], br.at[q], load_sem.at[8 + q])

    for q in range(4):
        load_b(q).start()
    for h in (1 - core, core):
        for g in range(4):
            load(g, h).start()

    barrier = pltpu.get_barrier_semaphore()
    sibling = device(x_lo, z, y, x_hi, 1 - core)
    partners = [device(x_lo, (z + dz) % 4, y, x_hi, core) for dz in range(1, 4)] + [
        device((x + dx) % 4 % 2, z, (y + dy) % 4, (x + dx) % 4 // 2, core)
        for dx in range(4) for dy in range(4) if (dx, dy) != (0, 0)
    ] + [sibling]
    for partner in partners:
        pl.semaphore_signal(barrier, inc=1, device_id=partner, device_id_type=MESH)

    for q in range(4):
        load_b(q).wait()

    def mask_b(q, carry):
        for d in range(11):
            for h in range(2):
                u = (16 - d) % 16
                bp[(q + d) % 2, 6 * q + d // 2, h] = masked(br[q, 16 * h + u], bm[q, 16 * h + u])
        bp[(q + 1) % 2, 6 * q + 5] = jnp.zeros((2, BS, BS), jnp.bfloat16)
        return carry

    lax.fori_loop(0, 4, mask_b, 0)
    pl.semaphore_wait(barrier, len(partners))
    send(bp.at[1 - core], bp.at[2], bp_s, bp_r, sibling)

    def mask_a(g, h):
        q = (z + ZORDER[g]) % 4
        load(g, h).wait()

        def one(t, carry):
            ar[q, h, t] = masked(ar[q, h, t], am[q, 16 * h + t])
            return carry

        lax.fori_loop(0, 16, one, 0)

    for g in range(4):
        mask_a(g, 1 - core)
        q = (z + ZORDER[g]) % 4
        send(ar.at[q, 1 - core], sa.at[q], sa_s, sa_r.at[g], sibling)

    def toward(near, carry, mine):
        for dx in range(4):
            for dy in range(4):
                to_x, to_y = (x + dx) % 4, (y + dy) % 4
                to_lo, to_hi = to_x % 2, to_x // 2
                d = near + 4 * to_lo
                inner = (4 * to_y + 2 * to_hi + core + d) % 16
                wanted = 2 * x_hi + (core if mine else 1 - core)

                @pl.when(inner // 4 == wanted)
                def _(dx=dx, dy=dy, to_lo=to_lo, to_y=to_y, to_hi=to_hi, d=d, inner=inner):
                    src = bp.at[core if mine else 2, 6 * (inner % 4) + d // 2]
                    dst = b1.at[near, x_lo * 4 + y]
                    if (dx, dy) == (0, 0):
                        pltpu.make_async_copy(src, dst, b1_r.at[near]).start()
                    else:
                        send(src, dst, b1_s, b1_r.at[near], device(to_lo, z, to_y, to_hi, core))
        return carry

    lax.fori_loop(0, 7, functools.partial(toward, mine=True), 0)

    def along(g, source, cs):
        to_z = (z + ZORDER[g]) % 4
        if g == 0:
            pltpu.make_async_copy(source, a1.at[z, cs], a1_sem.at[0]).start()
        else:
            back = ZORDER.index((4 - ZORDER[g]) % 4)
            for part in range(4):
                at = pl.ds(4 * part, 4)
                send(source.at[at], a1.at[z, cs, at], az_s, a1_sem.at[back], device(x_lo, to_z, y, x_hi, core))

    for g in (1, 2, 3, 0):
        mask_a(g, core)
        along(g, ar.at[(z + ZORDER[g]) % 4, core], core)
    for g in (0, 1, 2, 3):
        to_z = (z + ZORDER[g]) % 4
        wait_blocks(sa.at[to_z], sa_r.at[g])
        along(g, sa.at[to_z], 1 - core)

    wait_blocks(bp.at[2], bp_r)
    lax.fori_loop(0, 7, functools.partial(toward, mine=False), 0)

    def lift(near):
        wait_blocks(b1.at[near], b1_r.at[near])
        for dz in (1, 3, 2, 0):
            to_z = (z + dz) % 4
            step = near - to_z
            wanted = jnp.logical_and(step >= 0, step < 4)
            if dz == 2:
                wanted = jnp.logical_or(
                    jnp.logical_and(to_z == 0, near == 0), jnp.logical_and(to_z == 3, near == 6)
                )

            @pl.when(wanted)
            def _(dz=dz, to_z=to_z, step=step):
                step = jnp.clip(step, 0, 3)
                dst = b2.at[z, step]
                to = device(x_lo, to_z, y, x_hi, core)
                if dz == 0:
                    pltpu.make_async_copy(b1.at[near], dst, b2_r).start()
                elif dz == 2:
                    send(b1.at[near], dst, far_s, b2_r, to)
                else:
                    send(b1.at[near], dst, b2_s, near_r.at[dz // 2, step], to)

    def hand_on(way):
        from_z, to_z = ((z + 3) % 4, (z + 1) % 4) if way == 0 else ((z + 1) % 4, (z + 3) % 4)
        for step in range(4):
            wait_blocks(b2.at[0, 0], near_r.at[way, step])
            near = step + z
            if way == 0:
                low = jnp.where(to_z == 0, 3, jnp.where(to_z == 3, 4, to_z))
                high = jnp.where(to_z == 0, 3, jnp.where(to_z == 3, 5, to_z + 1))
            else:
                low = jnp.where(to_z == 0, 1, jnp.where(to_z == 3, 3, to_z + 2))
                high = jnp.where(to_z == 0, 2, jnp.where(to_z == 3, 3, to_z + 3))

            @pl.when(jnp.logical_and(near >= low, near <= high))
            def _(step=step, near=near):
                dst = b2.at[from_z, jnp.clip(near - to_z, 0, 3)]
                send(b2.at[from_z, step], dst, far_s, b2_r, device(x_lo, to_z, y, x_hi, core))

    def rows_from(zs, half):
        return pl.ds(half * 32 + zs * 8, 8)

    def land(index, m, src, sem, to):
        def put(dst):
            if to is None:
                pltpu.make_async_copy(src, dst, sem).start()
            else:
                send(src, dst, ax_s, sem, to)

        @pl.when(index == 4 * (1 - core))
        def _():
            put(spare.at[m])

        @pl.when(index != 4 * (1 - core))
        def _():
            put(left.at[core, m, jnp.clip(index - core, 0, 3)])

    def outer_sem(index, half):
        return jnp.where(jnp.logical_and(half == 1, index % 4 == 0), 5 + index // 4, index)

    def along_y(g):
        zs = (z + ZORDER[g]) % 4
        wait_blocks(a1.at[zs], a1_sem.at[g])
        for k in range(3):
            for cs in range(2):
                for dy in (1, 3, 2, 0):
                    to_y = (y + dy) % 4
                    src = a1.at[zs, cs, (4 * to_y + 2 + k + 8 * x_hi) % 16]
                    dst = ay.at[zs, y, cs, k]
                    if dy == 0:
                        pltpu.make_async_copy(src, dst, ay_r.at[g]).start()
                    else:
                        send(src, dst, ay_s, ay_r.at[g], device(x_lo, z, to_y, x_hi, core))

    def along_x(g):
        zs = (z + ZORDER[g]) % 4
        wait_blocks(ay.at[zs], ay_r.at[g])

        def one(from_y, carry):
            m = x_lo * 32 + zs * 8 + from_y * 2 + x_hi
            for k in (0, 2, 1):
                for dx in (1, 3, 2, 0):
                    to_x = (x + dx) % 4
                    to_lo, to_hi = to_x % 2, to_x // 2
                    index = k + 2 * (1 - to_hi)
                    to = None if dx == 0 else device(to_lo, z, y, to_hi, core)
                    src = ay.at[zs, from_y, to_lo, k]
                    if k == 1:
                        land(index, m, src, a2_sem.at[g, index], to)
                    else:
                        relayed = jnp.logical_and(x_lo == 1, to_hi == (0 if k == 2 else 1))

                        @pl.when(jnp.logical_not(relayed))
                        def _(index=index, src=src, to=to):
                            land(index, m, src, a2_sem.at[g, outer_sem(index, x_lo)], to)
            return carry

        lax.fori_loop(0, 4, one, 0)

    def direct(g):
        zs = (z + ZORDER[g]) % 4
        m = x_lo * 32 + zs * 8 + y * 2 + x_hi

        def column(outer):
            for dx in range(4):
                for dy in range(4):
                    to_x, to_y = (x + dx) % 4, (y + dy) % 4
                    to_lo, to_hi = to_x % 2, to_x // 2
                    index = 4 * to_hi if outer else 1 + 2 * to_hi
                    src = a1.at[zs, to_lo, (4 * to_y + 2 * to_hi + index + 8 * x_hi) % 16]
                    to = None if (dx, dy) == (0, 0) else device(to_lo, z, to_y, to_hi, core)
                    land(index, m, src, a2_sem.at[g, outer_sem(index, x_lo)], to)

        column(False)

        @pl.when(x_lo == 1)
        def _():
            column(True)

    def relay(g):
        zs = (z + ZORDER[g]) % 4
        for half in range(2):
            side = (x_hi + half) % 2
            wait_blocks(spare.at[pl.ds(0, 8)], a2_sem.at[g, outer_sem(4 * (1 - side), half)])
            to = device(x_lo, z, (y + 1 + 2 * side) % 4, x_hi, core)
            sem = a2_sem.at[g, outer_sem(4 * side, half)]
            rows = rows_from(zs, half)
            mine, other = left.at[core, rows, 3 * core], spare.at[rows]

            @pl.when(core == side)
            def _(mine=mine, other=other, sem=sem, to=to):
                send(other, mine, relay_s, sem, to)

            @pl.when(core != side)
            def _(mine=mine, other=other, sem=sem, to=to):
                send(mine, other, relay_s, sem, to)

    def share(g):
        zs = (z + ZORDER[g]) % 4
        for index in (2, 1, 3, 0):
            if index == 0:
                for half in range(2):
                    side = (x_hi + half) % 2
                    wait_blocks(spare.at[pl.ds(0, 8)], a2_sem.at[g, outer_sem(4 * side, half)])
            else:
                wait_blocks(spare.at[pl.ds(0, 16)], a2_sem.at[g, index])
            for half in range(2):
                rows = rows_from(zs, half)
                if index == 0:
                    send(spare.at[rows], left.at[core, rows, 3 * (1 - core)], a3_s, a3_r.at[g], sibling)
                else:
                    send(
                        left.at[core, rows, index - core], left.at[core, rows, index - 1 + core],
                        a3_s, a3_r.at[g], sibling,
                    )

    col = 4 * y + 2 * x_hi + core
    row = 4 * x_lo + z

    def result(g, half):
        slot = 2 * (g % 2) + half
        first_row = 32 * half + 8 * ((z + ZORDER[g]) % 4)
        return pltpu.make_async_copy(br.at[slot], out.at[pl.ds(4 * first_row, 32)], out_sem.at[slot])

    def multiply(g):
        zs = (z + ZORDER[g]) % 4
        wait_blocks(left.at[0, pl.ds(0, 16)], a3_r.at[g])

        def eight(half, carry):
            group = 16 * half + 4 * zs

            def four(odd, carry):
                before = None
                for j in range(-1, 4):
                    weights = []
                    for s in range(4):
                        offset = (col + s + 8 * odd) % 16
                        d = row + s
                        later = jnp.where(jnp.logical_and(offset >= d, d > 0), 0, 1)
                        n = (group + j + (8 * odd + row + offset) // 16 + 32) % 32
                        pair = b2.at[(n // 4) % 4, s, (n // 16) * 4 + n % 4]
                        weights.append(jnp.concatenate(
                            [masked(pair[0], later), pair[later], masked(pair[1], 1 - later)], axis=1
                        ))
                    lines = []
                    if j >= 0:
                        lines.append(jnp.concatenate([left[1, 2 * (group + j) + odd, s] for s in range(4)], axis=1))
                    if j < 3:
                        lines.append(jnp.concatenate([left[0, 2 * (group + j) + 2 + odd, s] for s in range(4)], axis=1))
                    part = jnp.dot(
                        jnp.concatenate(lines, axis=0), jnp.concatenate(weights, axis=0),
                        preferred_element_type=jnp.float32,
                    )
                    if j >= 0:
                        here = part[:BS]
                        sums = [
                            before[:, :BS],
                            before[:, BS:2 * BS] + here[:, :BS],
                            before[:, 2 * BS:] + here[:, BS:2 * BS],
                            here[:, 2 * BS:],
                        ]
                        for l in range(4):
                            br[2 * (g % 2) + half, 4 * (2 * j + odd) + l] = sums[l].astype(br.dtype)
                    before = part[-BS:]
                return carry

            if g >= 2:
                result(g - 2, half).wait()
            lax.fori_loop(0, 2, four, 0)
            result(g, half).start()
            return carry

        lax.fori_loop(0, 2, eight, 0)

    along_y(0)
    along_x(0)
    lift(0)
    lift(1)
    lift(2)
    lift(3)
    lift(4)
    along_y(1)
    along_y(2)
    lift(5)
    lift(6)
    along_y(3)
    along_x(1)
    direct(0)
    direct(1)
    along_x(2)
    direct(2)
    direct(3)
    relay(0)
    share(0)
    hand_on(0)
    hand_on(1)
    along_x(3)
    relay(1)
    share(1)
    relay(2)
    share(2)
    wait_blocks(b2.at[pl.ds(0, 2)], b2_r)
    multiply(0)
    multiply(1)
    relay(3)
    share(3)
    multiply(2)
    multiply(3)

    for g in (2, 3):
        for half in range(2):
            result(g, half).wait()
    wait_blocks(bp.at[0], bp_s)
    wait_blocks(sa, sa_s)
    wait_blocks(left.at[0], a3_s)
    wait_blocks(b2.at[pl.ds(0, 2)], b2_s)
    inner_z = jnp.logical_or(z == 1, z == 2)
    for inner, count in ((True, 5), (False, 3)):
        @pl.when(inner_z == inner)
        def _(count=count):
            wait_blocks(b1.at[pl.ds(0, count)], far_s)

    wait_blocks(left.at[0, pl.ds(0, 24)], az_s)
    wait_blocks(left.at[0, pl.ds(0, 18)], ay_s)
    for half, count in ((0, 51), (1, 54)):
        @pl.when(x_lo == half)
        def _(count=count):
            wait_blocks(left.at[0, pl.ds(0, count)], ax_s)

    wait_blocks(spare, relay_s)
    own = 0
    for near in range(7):
        inner = (col + 4 * x_lo + near) % 16
        own = own + jnp.where(inner // 8 == x_hi, 1, 0)
    for count in range(8):
        @pl.when(own == count)
        def _(count=count):
            wait_blocks(left.at[0, pl.ds(0, 56 - count), pl.ds(0, 2)], b1_s)


def product(a, am, b, bm):
    block = (BS, BS)
    hbm = pl.BlockSpec(memory_space=pl.ANY)
    smem = pl.BlockSpec(memory_space=pltpu.SMEM)
    stages = [
        (2, 64, 4), (4, 4, 8, 2), (4, 2, 16), (4, 32), (4, 2, 16), (4, 4, 2, 3), (4, 16), (3, 24, 2), (7, 8, 2), (64,)
    ]
    semaphores = [(12,), (12,), (4,), (4,), (4,), (7,), (4, 7), (2, 4), (4,), (4,)]
    out = pl.pallas_call(
        product_kernel,
        out_shape=jax.ShapeDtypeStruct((256,) + block, jnp.bfloat16),
        in_specs=[hbm, smem, hbm, smem],
        out_specs=hbm,
        scratch_shapes=[pltpu.VMEM(stage + block, jnp.bfloat16) for stage in stages]
        + [pltpu.SemaphoreType.DMA(shape) for shape in semaphores],
        compiler_params=pltpu.CompilerParams(collective_id=0, has_side_effects=True, vmem_limit_bytes=VMEM),
        name="exchange",
    )(a, am, b, bm)
    return out.reshape((64, 4) + block)


def deliver_kernel(src, dst):
    dst[...] = src[...]


def deliver(blocks):
    spec = pl.BlockSpec((8,) + blocks.shape[1:], lambda i: (i, 0, 0, 0))
    return pl.pallas_call(
        deliver_kernel,
        grid=(blocks.shape[0] // 8,),
        out_shape=jax.ShapeDtypeStruct(blocks.shape, blocks.dtype),
        in_specs=[spec],
        out_specs=spec,
        compiler_params=pltpu.CompilerParams(vmem_limit_bytes=VMEM),
        name="deliver",
    )(blocks)


def local(a_band, a_mask, b_band, b_mask):
    return deliver(product(a_band, a_mask, b_band, b_mask))


def solution(mesh):
    return jax.shard_map(
        local,
        mesh=mesh,
        in_specs=(
            P(("row", "col"), None, None, None),
            P(("row", "col"), None),
            P(("row", "col"), None, None, None),
            P(("row", "col"), None),
        ),
        out_specs=P("row", "col", None, None),
        check_vma=False,
    )
```

```python
import functools

import jax
import jax.numpy as jnp
from jax import lax
from jax.experimental import pallas as pl
from jax.experimental.pallas import tpu as pltpu
from jax.sharding import PartitionSpec as P

MESH = pl.DeviceIdType.MESH
BS = 128
ZORDER = (0, 1, 3, 2)
GROUP = 8
EXCHANGE_VMEM = 58 * 2**20
PRODUCT_VMEM = 58 * 2**20


def coords():
    row, col = lax.axis_index("row"), lax.axis_index("col")
    return row // 4, row % 4, col // 4, (col // 2) % 2, col % 2


def device(x_lo, z, y, x_hi, core):
    return (x_lo * 4 + z, y * 4 + x_hi * 2 + core)


def exchange_kernel(
    a, am, b, bm, left, b2, ar, br, a1, ay, sa, bp, b1, spare,
    sems, load_sem, a1_sem, ay_r, sa_r, b1_r, a2_sem
):
    x_lo, z, y, x_hi, core = coords()
    x = 2 * x_hi + x_lo
    (bp_s, bp_r, sa_s, az_s, b1_s, ax_s, b2_s, b2_r, a3_s, a3_r, ay_s, relay_s) = [
        sems.at[i] for i in range(12)
    ]

    def send(src, dst, send_sem, recv_sem, to):
        pltpu.make_async_remote_copy(
            src_ref=src, dst_ref=dst, send_sem=send_sem, recv_sem=recv_sem,
            device_id=to, device_id_type=MESH,
        ).start()

    def wait_blocks(ref, sem):
        pltpu.make_async_copy(ref, ref, sem).wait()

    def masked(block, keep):
        factor = jnp.full((16, BS), keep.astype(jnp.float32)).astype(jnp.bfloat16)
        return (block.reshape(BS // 16, 16, BS) * factor[None]).reshape(BS, BS)

    def load(g, h):
        q = (z + ZORDER[g]) % 4
        return pltpu.make_async_copy(a.at[q, pl.ds(16 * h, 16)], ar.at[q, h], load_sem.at[2 * g + (h + core) % 2])

    def load_b(q):
        return pltpu.make_async_copy(b.at[q], br.at[q], load_sem.at[8 + q])

    for q in range(4):
        load_b(q).start()
    for h in (1 - core, core):
        for g in range(4):
            load(g, h).start()

    barrier = pltpu.get_barrier_semaphore()
    sibling = device(x_lo, z, y, x_hi, 1 - core)
    partners = [device(x_lo, (z + dz) % 4, y, x_hi, core) for dz in range(1, 4)] + [
        device((x + dx) % 4 % 2, z, (y + dy) % 4, (x + dx) % 4 // 2, core)
        for dx in range(4) for dy in range(4) if (dx, dy) != (0, 0)
    ] + [sibling]
    for partner in partners:
        pl.semaphore_signal(barrier, inc=1, device_id=partner, device_id_type=MESH)

    for q in range(4):
        load_b(q).wait()

    def mask_b(q, carry):
        for d in range(11):
            for h in range(2):
                u = (16 - d) % 16
                bp[(q + d) % 2, 6 * q + d // 2, h] = masked(br[q, 16 * h + u], bm[q, 16 * h + u])
        bp[(q + 1) % 2, 6 * q + 5] = jnp.zeros((2, BS, BS), jnp.bfloat16)
        return carry

    lax.fori_loop(0, 4, mask_b, 0)
    pl.semaphore_wait(barrier, len(partners))
    send(bp.at[1 - core], bp.at[2], bp_s, bp_r, sibling)

    def mask_a(g, h):
        q = (z + ZORDER[g]) % 4
        load(g, h).wait()

        def one(t, carry):
            ar[q, h, t] = masked(ar[q, h, t], am[q, 16 * h + t])
            return carry

        lax.fori_loop(0, 16, one, 0)

    for g in range(4):
        mask_a(g, 1 - core)
        q = (z + ZORDER[g]) % 4
        send(ar.at[q, 1 - core], sa.at[q], sa_s, sa_r.at[g], sibling)

    def toward(near, carry, mine):
        for dx in range(4):
            for dy in range(4):
                to_x, to_y = (x + dx) % 4, (y + dy) % 4
                to_lo, to_hi = to_x % 2, to_x // 2
                d = near + 4 * to_lo
                inner = (4 * to_y + 2 * to_hi + core + d) % 16
                wanted = 2 * x_hi + (core if mine else 1 - core)

                @pl.when(inner // 4 == wanted)
                def _(dx=dx, dy=dy, to_lo=to_lo, to_y=to_y, to_hi=to_hi, d=d, inner=inner):
                    for h in range(2):
                        src = bp.at[core if mine else 2, 6 * (inner % 4) + d // 2, h]
                        dst = b1.at[near, x_lo * 4 + y, h]
                        if (dx, dy) == (0, 0):
                            pltpu.make_async_copy(src, dst, b1_r.at[near]).start()
                        else:
                            send(src, dst, b1_s, b1_r.at[near], device(to_lo, z, to_y, to_hi, core))
        return carry

    lax.fori_loop(0, 7, functools.partial(toward, mine=True), 0)

    def along(g, source, cs):
        to_z = (z + ZORDER[g]) % 4
        if g == 0:
            pltpu.make_async_copy(source, a1.at[z, cs], a1_sem.at[0]).start()
        else:
            back = ZORDER.index((4 - ZORDER[g]) % 4)
            for part in range(4):
                at = pl.ds(4 * part, 4)
                send(source.at[at], a1.at[z, cs, at], az_s, a1_sem.at[back], device(x_lo, to_z, y, x_hi, core))

    for g in (1, 2, 3, 0):
        mask_a(g, core)
        along(g, ar.at[(z + ZORDER[g]) % 4, core], core)
    for g in (0, 1, 2, 3):
        to_z = (z + ZORDER[g]) % 4
        wait_blocks(sa.at[to_z], sa_r.at[g])
        along(g, sa.at[to_z], 1 - core)

    wait_blocks(bp.at[2], bp_r)
    lax.fori_loop(0, 7, functools.partial(toward, mine=False), 0)

    def lift(near):
        wait_blocks(b1.at[near], b1_r.at[near])
        for dz in (1, 3, 2, 0):
            to_z = (z + dz) % 4
            step = near - to_z

            @pl.when(jnp.logical_and(step >= 0, step < 4))
            def _(dz=dz, to_z=to_z, step=step):
                dst = b2.at[z, jnp.clip(step, 0, 3)]
                if dz == 0:
                    pltpu.make_async_copy(b1.at[near], dst, b2_r).start()
                else:
                    send(b1.at[near], dst, b2_s, b2_r, device(x_lo, to_z, y, x_hi, core))

    def rows_from(zs, half):
        return pl.ds(half * 32 + zs * 8, 8)

    def land(index, m, src, sem, to):
        def put(dst):
            if to is None:
                pltpu.make_async_copy(src, dst, sem).start()
            else:
                send(src, dst, ax_s, sem, to)

        @pl.when(index == 4 * (1 - core))
        def _():
            put(spare.at[m])

        @pl.when(index != 4 * (1 - core))
        def _():
            put(left.at[core, m, jnp.clip(index - core, 0, 3)])

    def outer_sem(index, half):
        return jnp.where(jnp.logical_and(half == 1, index % 4 == 0), 5 + index // 4, index)

    def along_y(g):
        zs = (z + ZORDER[g]) % 4
        wait_blocks(a1.at[zs], a1_sem.at[g])
        for k in range(3):
            for cs in range(2):
                for dy in (1, 3, 2, 0):
                    to_y = (y + dy) % 4
                    src = a1.at[zs, cs, (4 * to_y + 2 + k + 8 * x_hi) % 16]
                    dst = ay.at[zs, y, cs, k]
                    if dy == 0:
                        pltpu.make_async_copy(src, dst, ay_r.at[g]).start()
                    else:
                        send(src, dst, ay_s, ay_r.at[g], device(x_lo, z, to_y, x_hi, core))

    def along_x(g):
        zs = (z + ZORDER[g]) % 4
        wait_blocks(ay.at[zs], ay_r.at[g])

        def one(from_y, carry):
            m = x_lo * 32 + zs * 8 + from_y * 2 + x_hi
            for k in (0, 2, 1):
                for dx in (1, 3, 2, 0):
                    to_x = (x + dx) % 4
                    to_lo, to_hi = to_x % 2, to_x // 2
                    index = k + 2 * (1 - to_hi)
                    to = None if dx == 0 else device(to_lo, z, y, to_hi, core)
                    src = ay.at[zs, from_y, to_lo, k]
                    if k == 1:
                        land(index, m, src, a2_sem.at[g, index], to)
                    else:
                        relayed = jnp.logical_and(x_lo == 1, to_hi == (0 if k == 2 else 1))

                        @pl.when(jnp.logical_not(relayed))
                        def _(index=index, src=src, to=to):
                            land(index, m, src, a2_sem.at[g, outer_sem(index, x_lo)], to)
            return carry

        lax.fori_loop(0, 4, one, 0)

    def direct(g):
        zs = (z + ZORDER[g]) % 4
        m = x_lo * 32 + zs * 8 + y * 2 + x_hi

        def column(outer):
            for dx in range(4):
                for dy in range(4):
                    to_x, to_y = (x + dx) % 4, (y + dy) % 4
                    to_lo, to_hi = to_x % 2, to_x // 2
                    index = 4 * to_hi if outer else 1 + 2 * to_hi
                    src = a1.at[zs, to_lo, (4 * to_y + 2 * to_hi + index + 8 * x_hi) % 16]
                    to = None if (dx, dy) == (0, 0) else device(to_lo, z, to_y, to_hi, core)
                    land(index, m, src, a2_sem.at[g, outer_sem(index, x_lo)], to)

        column(False)

        @pl.when(x_lo == 1)
        def _():
            column(True)

    def relay(g):
        zs = (z + ZORDER[g]) % 4
        for half in range(2):
            side = (x_hi + half) % 2
            wait_blocks(spare.at[pl.ds(0, 8)], a2_sem.at[g, outer_sem(4 * (1 - side), half)])
            to = device(x_lo, z, (y + 1 + 2 * side) % 4, x_hi, core)
            sem = a2_sem.at[g, outer_sem(4 * side, half)]
            rows = rows_from(zs, half)
            mine, other = left.at[core, rows, 3 * core], spare.at[rows]

            @pl.when(core == side)
            def _(mine=mine, other=other, sem=sem, to=to):
                send(other, mine, relay_s, sem, to)

            @pl.when(core != side)
            def _(mine=mine, other=other, sem=sem, to=to):
                send(mine, other, relay_s, sem, to)

    def share(g):
        zs = (z + ZORDER[g]) % 4
        for index in (2, 1, 3, 0):
            if index == 0:
                for half in range(2):
                    side = (x_hi + half) % 2
                    wait_blocks(spare.at[pl.ds(0, 8)], a2_sem.at[g, outer_sem(4 * side, half)])
            else:
                wait_blocks(spare.at[pl.ds(0, 16)], a2_sem.at[g, index])
            for half in range(2):
                rows = rows_from(zs, half)
                if index == 0:
                    send(spare.at[rows], left.at[core, rows, 3 * (1 - core)], a3_s, a3_r, sibling)
                else:
                    send(
                        left.at[core, rows, index - core], left.at[core, rows, index - 1 + core],
                        a3_s, a3_r, sibling,
                    )

    along_y(0)
    along_x(0)
    lift(0)
    lift(1)
    lift(2)
    lift(3)
    lift(4)
    along_y(1)
    along_y(2)
    lift(5)
    lift(6)
    along_y(3)
    direct(0)
    along_x(1)
    direct(1)
    along_x(2)
    direct(2)
    direct(3)
    relay(0)
    share(0)
    along_x(3)
    relay(1)
    share(1)
    relay(2)
    share(2)
    relay(3)
    share(3)

    wait_blocks(left.at[0], a3_r)
    wait_blocks(b2, b2_r)
    wait_blocks(bp.at[0], bp_s)
    wait_blocks(sa, sa_s)
    wait_blocks(left.at[0], a3_s)
    wait_blocks(b2.at[pl.ds(0, 3)], b2_s)
    wait_blocks(left.at[0, pl.ds(0, 24)], az_s)
    wait_blocks(left.at[0, pl.ds(0, 18)], ay_s)
    for half, count in ((0, 51), (1, 54)):
        @pl.when(x_lo == half)
        def _(count=count):
            wait_blocks(left.at[0, pl.ds(0, count)], ax_s)

    wait_blocks(spare, relay_s)
    col = 4 * y + 2 * x_hi + core
    own = 0
    for near in range(7):
        inner = (col + 4 * x_lo + near) % 16
        own = own + jnp.where(inner // 8 == x_hi, 1, 0)
    for count in range(8):
        @pl.when(own == count)
        def _(count=count):
            wait_blocks(left.at[0, pl.ds(0, 56 - count), pl.ds(0, 2)], b1_s)


def exchange(a, am, b, bm):
    block = (BS, BS)
    hbm = pl.BlockSpec(memory_space=pl.ANY)
    smem = pl.BlockSpec(memory_space=pltpu.SMEM)
    shapes = [(2, 64, 4), (4, 4, 8, 2)]
    stages = [(4, 2, 16), (4, 32), (4, 2, 16), (4, 4, 2, 3), (4, 16), (3, 24, 2), (7, 8, 2), (64,)]
    semaphores = [(12,), (12,), (4,), (4,), (4,), (7,), (4, 7)]
    return pl.pallas_call(
        exchange_kernel,
        out_shape=[jax.ShapeDtypeStruct(shape + block, jnp.bfloat16) for shape in shapes],
        in_specs=[hbm, smem, hbm, smem],
        out_specs=[hbm] * len(shapes),
        scratch_shapes=[pltpu.VMEM(stage + block, jnp.bfloat16) for stage in stages]
        + [pltpu.SemaphoreType.DMA(shape) for shape in semaphores],
        compiler_params=pltpu.CompilerParams(
            collective_id=0, has_side_effects=True, vmem_limit_bytes=EXCHANGE_VMEM
        ),
        name="exchange",
    )(a, am, b, bm)


def product_kernel(left, b2, out, right, sems):
    x_lo, z, y, x_hi, core = coords()
    col = 4 * y + 2 * x_hi + core
    row = 4 * x_lo + z
    i = pl.program_id(0)

    def fetch(n):
        return pltpu.make_async_copy(
            b2.at[(n // 4) % 4, :, (n // 16) * 4 + n % 4], right.at[n, :, pl.ds(1, 2)], sems.at[n]
        )

    def ready(n):
        fetch(n).wait()
        for s in range(4):
            right[n, s, 0] = jnp.zeros((BS, BS), jnp.bfloat16)
            right[n, s, 3] = jnp.zeros((BS, BS), jnp.bfloat16)

    @pl.when(i == 0)
    def _():
        def begin(n, carry):
            fetch((n + 31) % 32).start()
            return carry

        lax.fori_loop(0, 32, begin, 0)
        ready(31)
        ready(0)

    for j in range(1, GROUP + 1):
        n = i * GROUP + j
        pl.when(n < 31)(functools.partial(ready, n))

    for odd in range(2):
        before = None
        for j in range(-1, GROUP):
            weights = []
            for s in range(4):
                offset = (col + s + 8 * odd) % 16
                d = row + s
                first = jnp.where(jnp.logical_and(offset >= d, d > 0), 0, 1)
                n = (i * GROUP + j + (8 * odd + row + offset) // 16 + 32) % 32
                weights.append(jnp.concatenate([right[n, s, first + l] for l in range(3)], axis=1))
            lines = []
            if j >= 0:
                lines.append(jnp.concatenate([left[1, 2 * j + odd, s] for s in range(4)], axis=1))
            if j < GROUP - 1:
                lines.append(jnp.concatenate([left[0, 2 * j + 2 + odd, s] for s in range(4)], axis=1))
            part = jnp.dot(
                jnp.concatenate(lines, axis=0), jnp.concatenate(weights, axis=0), preferred_element_type=jnp.float32
            )
            if j >= 0:
                here = part[:BS]
                sums = [
                    before[:, :BS],
                    before[:, BS:2 * BS] + here[:, :BS],
                    before[:, 2 * BS:] + here[:, BS:2 * BS],
                    here[:, 2 * BS:],
                ]
                for l in range(4):
                    out[2 * j + odd, l] = sums[l].astype(out.dtype)
            before = part[-BS:]


def product(left, b2):
    block = (BS, BS)
    return pl.pallas_call(
        product_kernel,
        grid=(32 // GROUP,),
        out_shape=jax.ShapeDtypeStruct((64, 4) + block, jnp.bfloat16),
        in_specs=[
            pl.BlockSpec((2, 2 * GROUP, 4) + block, lambda i: (0, i, 0, 0, 0)),
            pl.BlockSpec(memory_space=pl.ANY),
        ],
        out_specs=pl.BlockSpec((2 * GROUP, 4) + block, lambda i: (i, 0, 0, 0)),
        scratch_shapes=[pltpu.VMEM((32, 4, 4) + block, jnp.bfloat16), pltpu.SemaphoreType.DMA((32,))],
        compiler_params=pltpu.CompilerParams(vmem_limit_bytes=PRODUCT_VMEM),
        name="product",
    )(left, b2)


def local(a_band, a_mask, b_band, b_mask):
    left, right = exchange(a_band, a_mask, b_band, b_mask)
    return product(left, right)


def solution(mesh):
    return jax.shard_map(
        local,
        mesh=mesh,
        in_specs=(
            P(("row", "col"), None, None, None),
            P(("row", "col"), None),
            P(("row", "col"), None, None, None),
            P(("row", "col"), None),
        ),
        out_specs=P("row", "col", None, None),
        check_vma=False,
    )
```

```python
import functools

import jax
import jax.numpy as jnp
from jax import lax
from jax.experimental import pallas as pl
from jax.experimental.pallas import tpu as pltpu
from jax.sharding import PartitionSpec as P

MESH = pl.DeviceIdType.MESH
BS = 128
ZORDER = (0, 1, 3, 2)
VMEM = 58 * 2**20


def coords():
    row, col = lax.axis_index("row"), lax.axis_index("col")
    return row // 4, row % 4, col // 4, (col // 2) % 2, col % 2


def device(x_lo, z, y, x_hi, core):
    return (x_lo * 4 + z, y * 4 + x_hi * 2 + core)


def product_kernel(
    a, am, b, bm, out, left, b2, ar, br, a1, ay, sa, bp, b1, spare,
    sems, load_sem, a1_sem, ay_r, sa_r, b1_r, a2_sem, near_r, a3_r, out_sem
):
    x_lo, z, y, x_hi, core = coords()
    x = 2 * x_hi + x_lo
    (bp_s, bp_r, sa_s, az_s, b1_s, ax_s, b2_s, b2_r, a3_s, ay_s, relay_s, far_s) = [
        sems.at[i] for i in range(12)
    ]

    def send(src, dst, send_sem, recv_sem, to):
        pltpu.make_async_remote_copy(
            src_ref=src, dst_ref=dst, send_sem=send_sem, recv_sem=recv_sem,
            device_id=to, device_id_type=MESH,
        ).start()

    def wait_blocks(ref, sem):
        pltpu.make_async_copy(ref, ref, sem).wait()

    def masked(block, keep):
        factor = jnp.full((16, BS), keep.astype(jnp.float32)).astype(jnp.bfloat16)
        return (block.reshape(BS // 16, 16, BS) * factor[None]).reshape(BS, BS)

    def load(g, h):
        q = (z + ZORDER[g]) % 4
        return pltpu.make_async_copy(a.at[q, pl.ds(16 * h, 16)], ar.at[q, h], load_sem.at[2 * g + (h + core) % 2])

    def load_b(q):
        return pltpu.make_async_copy(b.at[q], br.at[q], load_sem.at[8 + q])

    for q in range(4):
        load_b(q).start()
    for h in (1 - core, core):
        for g in range(4):
            load(g, h).start()

    barrier = pltpu.get_barrier_semaphore()
    sibling = device(x_lo, z, y, x_hi, 1 - core)
    partners = [device(x_lo, (z + dz) % 4, y, x_hi, core) for dz in range(1, 4)] + [
        device((x + dx) % 4 % 2, z, (y + dy) % 4, (x + dx) % 4 // 2, core)
        for dx in range(4) for dy in range(4) if (dx, dy) != (0, 0)
    ] + [sibling]
    for partner in partners:
        pl.semaphore_signal(barrier, inc=1, device_id=partner, device_id_type=MESH)

    for q in range(4):
        load_b(q).wait()

    def mask_b(q, carry):
        for d in range(11):
            for h in range(2):
                u = (16 - d) % 16
                bp[(q + d) % 2, 6 * q + d // 2, h] = masked(br[q, 16 * h + u], bm[q, 16 * h + u])
        bp[(q + 1) % 2, 6 * q + 5] = jnp.zeros((2, BS, BS), jnp.bfloat16)
        return carry

    lax.fori_loop(0, 4, mask_b, 0)
    pl.semaphore_wait(barrier, len(partners))
    send(bp.at[1 - core], bp.at[2], bp_s, bp_r, sibling)

    def mask_a(g, h):
        q = (z + ZORDER[g]) % 4
        load(g, h).wait()

        def one(t, carry):
            ar[q, h, t] = masked(ar[q, h, t], am[q, 16 * h + t])
            return carry

        lax.fori_loop(0, 16, one, 0)

    for g in range(4):
        mask_a(g, 1 - core)
        q = (z + ZORDER[g]) % 4
        send(ar.at[q, 1 - core], sa.at[q], sa_s, sa_r.at[g], sibling)

    def toward(near, carry, mine):
        for dx in range(4):
            for dy in range(4):
                to_x, to_y = (x + dx) % 4, (y + dy) % 4
                to_lo, to_hi = to_x % 2, to_x // 2
                d = near + 4 * to_lo
                inner = (4 * to_y + 2 * to_hi + core + d) % 16
                wanted = 2 * x_hi + (core if mine else 1 - core)

                @pl.when(inner // 4 == wanted)
                def _(dx=dx, dy=dy, to_lo=to_lo, to_y=to_y, to_hi=to_hi, d=d, inner=inner):
                    src = bp.at[core if mine else 2, 6 * (inner % 4) + d // 2]
                    dst = b1.at[near, x_lo * 4 + y]
                    if (dx, dy) == (0, 0):
                        pltpu.make_async_copy(src, dst, b1_r.at[near]).start()
                    else:
                        send(src, dst, b1_s, b1_r.at[near], device(to_lo, z, to_y, to_hi, core))
        return carry

    lax.fori_loop(0, 7, functools.partial(toward, mine=True), 0)

    def along(g, source, cs):
        to_z = (z + ZORDER[g]) % 4
        if g == 0:
            pltpu.make_async_copy(source, a1.at[z, cs], a1_sem.at[0]).start()
        else:
            back = ZORDER.index((4 - ZORDER[g]) % 4)
            for part in range(4):
                at = pl.ds(4 * part, 4)
                send(source.at[at], a1.at[z, cs, at], az_s, a1_sem.at[back], device(x_lo, to_z, y, x_hi, core))

    for g in (1, 2, 3, 0):
        mask_a(g, core)
        along(g, ar.at[(z + ZORDER[g]) % 4, core], core)
    for g in (0, 1, 2, 3):
        to_z = (z + ZORDER[g]) % 4
        wait_blocks(sa.at[to_z], sa_r.at[g])
        along(g, sa.at[to_z], 1 - core)

    wait_blocks(bp.at[2], bp_r)
    lax.fori_loop(0, 7, functools.partial(toward, mine=False), 0)

    def lift(near):
        wait_blocks(b1.at[near], b1_r.at[near])
        for dz in (1, 3, 2, 0):
            to_z = (z + dz) % 4
            step = near - to_z
            wanted = jnp.logical_and(step >= 0, step < 4)
            if dz == 2:
                wanted = jnp.logical_or(
                    jnp.logical_and(to_z == 0, near == 0), jnp.logical_and(to_z == 3, near == 6)
                )

            @pl.when(wanted)
            def _(dz=dz, to_z=to_z, step=step):
                step = jnp.clip(step, 0, 3)
                dst = b2.at[z, step]
                to = device(x_lo, to_z, y, x_hi, core)
                if dz == 0:
                    pltpu.make_async_copy(b1.at[near], dst, b2_r).start()
                elif dz == 2:
                    send(b1.at[near], dst, far_s, b2_r, to)
                else:
                    send(b1.at[near], dst, b2_s, near_r.at[dz // 2, step], to)

    def hand_on(way):
        from_z, to_z = ((z + 3) % 4, (z + 1) % 4) if way == 0 else ((z + 1) % 4, (z + 3) % 4)
        for step in range(4):
            wait_blocks(b2.at[0, 0], near_r.at[way, step])
            near = step + z
            if way == 0:
                low = jnp.where(to_z == 0, 3, jnp.where(to_z == 3, 4, to_z))
                high = jnp.where(to_z == 0, 3, jnp.where(to_z == 3, 5, to_z + 1))
            else:
                low = jnp.where(to_z == 0, 1, jnp.where(to_z == 3, 3, to_z + 2))
                high = jnp.where(to_z == 0, 2, jnp.where(to_z == 3, 3, to_z + 3))

            @pl.when(jnp.logical_and(near >= low, near <= high))
            def _(step=step, near=near):
                dst = b2.at[from_z, jnp.clip(near - to_z, 0, 3)]
                send(b2.at[from_z, step], dst, far_s, b2_r, device(x_lo, to_z, y, x_hi, core))

    def rows_from(zs, half):
        return pl.ds(half * 32 + zs * 8, 8)

    def land(index, m, src, sem, to):
        def put(dst):
            if to is None:
                pltpu.make_async_copy(src, dst, sem).start()
            else:
                send(src, dst, ax_s, sem, to)

        @pl.when(index == 4 * (1 - core))
        def _():
            put(spare.at[m])

        @pl.when(index != 4 * (1 - core))
        def _():
            put(left.at[core, m, jnp.clip(index - core, 0, 3)])

    def outer_sem(index, half):
        return jnp.where(jnp.logical_and(half == 1, index % 4 == 0), 5 + index // 4, index)

    def along_y(g):
        zs = (z + ZORDER[g]) % 4
        wait_blocks(a1.at[zs], a1_sem.at[g])
        for k in range(3):
            for cs in range(2):
                for dy in (1, 3, 2, 0):
                    to_y = (y + dy) % 4
                    src = a1.at[zs, cs, (4 * to_y + 2 + k + 8 * x_hi) % 16]
                    dst = ay.at[zs, y, cs, k]
                    if dy == 0:
                        pltpu.make_async_copy(src, dst, ay_r.at[g]).start()
                    else:
                        send(src, dst, ay_s, ay_r.at[g], device(x_lo, z, to_y, x_hi, core))

    def along_x(g):
        zs = (z + ZORDER[g]) % 4
        wait_blocks(ay.at[zs], ay_r.at[g])

        def one(from_y, carry):
            m = x_lo * 32 + zs * 8 + from_y * 2 + x_hi
            for k in (0, 2, 1):
                for dx in (1, 3, 2, 0):
                    to_x = (x + dx) % 4
                    to_lo, to_hi = to_x % 2, to_x // 2
                    index = k + 2 * (1 - to_hi)
                    to = None if dx == 0 else device(to_lo, z, y, to_hi, core)
                    src = ay.at[zs, from_y, to_lo, k]
                    if k == 1:
                        land(index, m, src, a2_sem.at[g, index], to)
                    else:
                        relayed = jnp.logical_and(x_lo == 1, to_hi == (0 if k == 2 else 1))

                        @pl.when(jnp.logical_not(relayed))
                        def _(index=index, src=src, to=to):
                            land(index, m, src, a2_sem.at[g, outer_sem(index, x_lo)], to)
            return carry

        lax.fori_loop(0, 4, one, 0)

    def direct(g):
        zs = (z + ZORDER[g]) % 4
        m = x_lo * 32 + zs * 8 + y * 2 + x_hi

        def column(outer):
            for dx in range(4):
                for dy in range(4):
                    to_x, to_y = (x + dx) % 4, (y + dy) % 4
                    to_lo, to_hi = to_x % 2, to_x // 2
                    index = 4 * to_hi if outer else 1 + 2 * to_hi
                    src = a1.at[zs, to_lo, (4 * to_y + 2 * to_hi + index + 8 * x_hi) % 16]
                    to = None if (dx, dy) == (0, 0) else device(to_lo, z, to_y, to_hi, core)
                    land(index, m, src, a2_sem.at[g, outer_sem(index, x_lo)], to)

        column(False)

        @pl.when(x_lo == 1)
        def _():
            column(True)

    def relay(g):
        zs = (z + ZORDER[g]) % 4
        for half in range(2):
            side = (x_hi + half) % 2
            wait_blocks(spare.at[pl.ds(0, 8)], a2_sem.at[g, outer_sem(4 * (1 - side), half)])
            to = device(x_lo, z, (y + 1 + 2 * side) % 4, x_hi, core)
            sem = a2_sem.at[g, outer_sem(4 * side, half)]
            rows = rows_from(zs, half)
            mine, other = left.at[core, rows, 3 * core], spare.at[rows]

            @pl.when(core == side)
            def _(mine=mine, other=other, sem=sem, to=to):
                send(other, mine, relay_s, sem, to)

            @pl.when(core != side)
            def _(mine=mine, other=other, sem=sem, to=to):
                send(mine, other, relay_s, sem, to)

    def share(g):
        zs = (z + ZORDER[g]) % 4
        for index in (2, 1, 3, 0):
            if index == 0:
                for half in range(2):
                    side = (x_hi + half) % 2
                    wait_blocks(spare.at[pl.ds(0, 8)], a2_sem.at[g, outer_sem(4 * side, half)])
            else:
                wait_blocks(spare.at[pl.ds(0, 16)], a2_sem.at[g, index])
            for half in range(2):
                rows = rows_from(zs, half)
                if index == 0:
                    send(spare.at[rows], left.at[core, rows, 3 * (1 - core)], a3_s, a3_r.at[g], sibling)
                else:
                    send(
                        left.at[core, rows, index - core], left.at[core, rows, index - 1 + core],
                        a3_s, a3_r.at[g], sibling,
                    )

    col = 4 * y + 2 * x_hi + core
    row = 4 * x_lo + z

    def result(g, half):
        slot = 2 * (g % 2) + half
        first_row = 32 * half + 8 * ((z + ZORDER[g]) % 4)
        return pltpu.make_async_copy(br.at[slot], out.at[pl.ds(4 * first_row, 32)], out_sem.at[slot])

    def multiply(g):
        zs = (z + ZORDER[g]) % 4
        wait_blocks(left.at[0, pl.ds(0, 16)], a3_r.at[g])

        def eight(half, carry):
            group = 16 * half + 4 * zs

            def four(odd, carry):
                before = None
                for j in range(-1, 4):
                    weights = []
                    for s in range(4):
                        offset = (col + s + 8 * odd) % 16
                        d = row + s
                        later = jnp.where(jnp.logical_and(offset >= d, d > 0), 0, 1)
                        n = (group + j + (8 * odd + row + offset) // 16 + 32) % 32
                        pair = b2.at[(n // 4) % 4, s, (n // 16) * 4 + n % 4]
                        weights.append(jnp.concatenate(
                            [masked(pair[0], later), pair[later], masked(pair[1], 1 - later)], axis=1
                        ))
                    lines = []
                    if j >= 0:
                        lines.append(jnp.concatenate([left[1, 2 * (group + j) + odd, s] for s in range(4)], axis=1))
                    if j < 3:
                        lines.append(jnp.concatenate([left[0, 2 * (group + j) + 2 + odd, s] for s in range(4)], axis=1))
                    part = jnp.dot(
                        jnp.concatenate(lines, axis=0), jnp.concatenate(weights, axis=0),
                        preferred_element_type=jnp.float32,
                    )
                    if j >= 0:
                        here = part[:BS]
                        sums = [
                            before[:, :BS],
                            before[:, BS:2 * BS] + here[:, :BS],
                            before[:, 2 * BS:] + here[:, BS:2 * BS],
                            here[:, 2 * BS:],
                        ]
                        for l in range(4):
                            br[2 * (g % 2) + half, 4 * (2 * j + odd) + l] = sums[l].astype(br.dtype)
                    before = part[-BS:]
                return carry

            if g >= 2:
                result(g - 2, half).wait()
            lax.fori_loop(0, 2, four, 0)
            result(g, half).start()
            return carry

        lax.fori_loop(0, 2, eight, 0)

    along_y(0)
    along_x(0)
    lift(0)
    lift(1)
    lift(2)
    lift(3)
    lift(4)
    along_y(1)
    along_y(2)
    lift(5)
    lift(6)
    along_y(3)
    along_x(1)
    direct(0)
    direct(1)
    along_x(2)
    direct(2)
    direct(3)
    relay(0)
    share(0)
    hand_on(0)
    hand_on(1)
    along_x(3)
    relay(1)
    share(1)
    relay(2)
    share(2)
    wait_blocks(b2.at[pl.ds(0, 2)], b2_r)
    multiply(0)
    multiply(1)
    relay(3)
    share(3)
    multiply(2)
    multiply(3)

    for g in (2, 3):
        for half in range(2):
            result(g, half).wait()
    wait_blocks(bp.at[0], bp_s)
    wait_blocks(sa, sa_s)
    wait_blocks(left.at[0], a3_s)
    wait_blocks(b2.at[pl.ds(0, 2)], b2_s)
    inner_z = jnp.logical_or(z == 1, z == 2)
    for inner, count in ((True, 5), (False, 3)):
        @pl.when(inner_z == inner)
        def _(count=count):
            wait_blocks(b1.at[pl.ds(0, count)], far_s)

    wait_blocks(left.at[0, pl.ds(0, 24)], az_s)
    wait_blocks(left.at[0, pl.ds(0, 18)], ay_s)
    for half, count in ((0, 51), (1, 54)):
        @pl.when(x_lo == half)
        def _(count=count):
            wait_blocks(left.at[0, pl.ds(0, count)], ax_s)

    wait_blocks(spare, relay_s)
    own = 0
    for near in range(7):
        inner = (col + 4 * x_lo + near) % 16
        own = own + jnp.where(inner // 8 == x_hi, 1, 0)
    for count in range(8):
        @pl.when(own == count)
        def _(count=count):
            wait_blocks(left.at[0, pl.ds(0, 56 - count), pl.ds(0, 2)], b1_s)


def product(a, am, b, bm):
    block = (BS, BS)
    hbm = pl.BlockSpec(memory_space=pl.ANY)
    smem = pl.BlockSpec(memory_space=pltpu.SMEM)
    stages = [
        (2, 64, 4), (4, 4, 8, 2), (4, 2, 16), (4, 32), (4, 2, 16), (4, 4, 2, 3), (4, 16), (3, 24, 2), (7, 8, 2), (64,)
    ]
    semaphores = [(12,), (12,), (4,), (4,), (4,), (7,), (4, 7), (2, 4), (4,), (4,)]
    out = pl.pallas_call(
        product_kernel,
        out_shape=jax.ShapeDtypeStruct((256,) + block, jnp.bfloat16),
        in_specs=[hbm, smem, hbm, smem],
        out_specs=hbm,
        scratch_shapes=[pltpu.VMEM(stage + block, jnp.bfloat16) for stage in stages]
        + [pltpu.SemaphoreType.DMA(shape) for shape in semaphores],
        compiler_params=pltpu.CompilerParams(collective_id=0, has_side_effects=True, vmem_limit_bytes=VMEM),
        name="exchange",
    )(a, am, b, bm)
    return out.reshape((64, 4) + block)


def deliver_kernel(src, dst, held, in_sem, out_sem):
    pieces = in_sem.shape[0]
    rows = src.shape[0] // pieces

    def into(i):
        at = pl.ds(i * rows, rows)
        return pltpu.make_async_copy(src.at[at], held.at[at], in_sem.at[i])

    def out_of(i):
        at = pl.ds(i * rows, rows)
        return pltpu.make_async_copy(held.at[at], dst.at[at], out_sem.at[i])

    for i in range(pieces):
        into(i).start()
    for i in range(pieces):
        into(i).wait()
        out_of(i).start()
    for i in range(pieces):
        out_of(i).wait()


def deliver(blocks):
    hbm = pl.BlockSpec(memory_space=pl.ANY)
    return pl.pallas_call(
        deliver_kernel,
        out_shape=jax.ShapeDtypeStruct(blocks.shape, blocks.dtype),
        in_specs=[hbm],
        out_specs=hbm,
        scratch_shapes=[
            pltpu.VMEM(blocks.shape, blocks.dtype), pltpu.SemaphoreType.DMA((16,)), pltpu.SemaphoreType.DMA((16,))
        ],
        compiler_params=pltpu.CompilerParams(vmem_limit_bytes=VMEM),
        name="deliver",
    )(blocks)


def local(a_band, a_mask, b_band, b_mask):
    return deliver(product(a_band, a_mask, b_band, b_mask))


def solution(mesh):
    return jax.shard_map(
        local,
        mesh=mesh,
        in_specs=(
            P(("row", "col"), None, None, None),
            P(("row", "col"), None),
            P(("row", "col"), None, None, None),
            P(("row", "col"), None),
        ),
        out_specs=P("row", "col", None, None),
        check_vma=False,
    )
```
